32 devices in a mesh: dp: 2 (over y), mp: 16 (over z, x, core).
Axes of the slice: x: 2, y: 2, z: 4, core: 2. Of those that a mesh axis runs over, the one named last changes fastest.
Arguments:
- dec_input: bfloat16 [2, 256, 4096], P('dp', None, 'mp'), may hold values from -6 to 6
- enc_output: bfloat16 [2, 256, 4096], P('dp', 'mp'), may hold values from -32 to 32
- query_weight: bfloat16 [4096, 4096], P('dp', 'mp'), may hold values from -3 to 3
- key_weight: bfloat16 [4096, 4096], P('dp', 'mp'), may hold values from -1 to 1
- value_weight: bfloat16 [4096, 4096], P('dp', 'mp'), may hold values from -0.09375 to 0.09375
- output_weight: bfloat16 [4096, 4096], P('mp', 'dp'), may hold values from -0.09375 to 0.09375
- cotangent: bfloat16 [2, 256, 4096], P('dp', None, 'mp'), may hold values from -6 to 6
- enc_lengths: int32 [2], P('dp'), may hold values from 64 to 256
- dec_lengths: int32 [2], P('dp'), may hold values from 64 to 256
Outputs:
- layer_out: bfloat16 [2, 256, 4096], P('dp', None, 'mp')
- input_grad: bfloat16 [2, 256, 4096], P('dp', None, 'mp')
- enc_grad: bfloat16 [2, 256, 4096], P('dp', 'mp')
- query_grad: bfloat16 [4096, 4096], P('dp', 'mp')
- key_grad: bfloat16 [4096, 4096], P('dp', 'mp')
- value_grad: bfloat16 [4096, 4096], P('dp', 'mp')
- output_grad: bfloat16 [4096, 4096], P('mp', 'dp')
The draws below stay inside these ranges and needn't reach their ends.
All inputs are finite; a program needn't handle non-finite values.
Results may differ from the reference program's by a relative error of at most 0.019.
The reference program's roundings to bfloat16 on the way (of `normed`, `probs_low`, `attended`, `masked`, `attended_grad` and `scores_grad`) count: a program that leaves them out, or rounds other values in their place, can miss the bound.
Values may be sent and summed in bfloat16 or wider, within the bound.
A program may use at most 64 MiB of HBM per device.

```python
import jax
import jax.numpy as jnp
from jax import lax

D = 4096
H = 16
DH = 256
TGT = 256
LENC = 256
SEQS = 2
N_MP = 16


def common_weight(key):
    source = jax.random.fold_in(key, 202)
    return jnp.clip(jax.random.normal(source, (D, D), jnp.float32), -4.0, 4.0) * D ** (-0.5)


def draw_dec_input(key, part):
    key = jax.random.fold_in(key, 7)
    values = jnp.clip(jax.random.normal(key, (SEQS, TGT, D), jnp.float32), -6.0, 6.0)
    return values.astype(jnp.bfloat16)


def draw_enc_output(key, part):
    key = jax.random.fold_in(key, 11)
    values = jnp.clip(jax.random.normal(key, (SEQS, LENC, D), jnp.float32), -4.0, 4.0)
    return values.astype(jnp.bfloat16)


def draw_query_weight(key, part):
    key = jax.random.fold_in(key, 13)
    values = jnp.clip(jax.random.normal(key, (D, D), jnp.float32), -4.0, 4.0) * D ** (-0.5)
    return values.astype(jnp.bfloat16)


def draw_key_weight(key, part):
    return common_weight(key).astype(jnp.bfloat16)


def level_of(own_key, extent, cuts, smallest, top_value):
    gain, own = 1.0, jax.random.fold_in(own_key, 6)
    for axis_at, blocks in cuts:
        heights = jnp.exp(jax.random.uniform(jax.random.fold_in(own, axis_at), (blocks,), jnp.float32, smallest / len(cuts), top_value / len(cuts)))
        gain = gain * jnp.repeat(heights, extent[axis_at] // blocks).reshape([-1 if axis == axis_at else 1 for axis in range(len(extent))])
    return gain


def gaussian(rng, dims, scale, bound, pieces=(), held_as=jnp.bfloat16):
    drawn = scale * jax.random.normal(rng, dims, jnp.float32)
    if pieces:
        drawn = drawn * level_of(rng, dims, pieces, -0.22, 0.18)
    return jnp.clip(drawn, -bound, bound).astype(held_as)


def setup_inputs(seed: int = 0) -> dict:
    keys = jax.random.split(jax.random.key(seed), 10)
    return {
        "dec_input": draw_dec_input(jax.random.fold_in(keys[9], 71), 0),
        "enc_output": draw_enc_output(jax.random.fold_in(keys[9], 71), 0),
        "query_weight": draw_query_weight(jax.random.fold_in(keys[9], 71), 0),
        "key_weight": draw_key_weight(jax.random.fold_in(keys[9], 71), 0),
        "value_weight": gaussian(keys[4], (D, D), D ** -0.5, 0.09375, ((0, 2), (1, 16))),
        "output_weight": gaussian(keys[5], (D, D), D ** -0.5, 0.09375, ((0, 16), (1, 2))),
        "cotangent": gaussian(keys[6], (SEQS, TGT, D), 1.0, 6.0, ((0, 2), (2, 16))),
        "enc_lengths": jax.random.randint(keys[7], (SEQS,), LENC // 4, LENC + 1).astype(jnp.int32),
        "dec_lengths": jax.random.randint(keys[8], (SEQS,), TGT // 4, TGT + 1).astype(jnp.int32),
    }


def round_sum(terms):
    rounded = lax.optimization_barrier(terms.astype(jnp.bfloat16))
    return lax.optimization_barrier(jnp.sum(rounded.astype(jnp.float32), axis=0))

def grouped(left, weight, groups):
    rows = left.shape[0]
    width = left.shape[1] // groups
    return jnp.einsum('rgk,gke->gre', left.reshape(rows, groups, width).astype(jnp.float32), weight.reshape(groups, width, weight.shape[1]).astype(jnp.float32))

def round_once(term):
    return lax.optimization_barrier(term.astype(jnp.bfloat16)).astype(jnp.float32)

def reference(dec_input, enc_output, query_weight, key_weight, value_weight, output_weight, cotangent, enc_lengths, dec_lengths):
    scale = DH ** (-0.5)

    def one_seq(totals, inputs):
        hidden, encoded, upstream, enc_len, dec_len = inputs
        hidden32 = hidden.astype(jnp.float32)
        inv_rms = lax.rsqrt(lax.optimization_barrier(jnp.mean(hidden32 * hidden32, axis=-1, keepdims=True)) + 1e-06)
        normed = (hidden32 * inv_rms).astype(jnp.bfloat16)
        query = jnp.dot(normed, query_weight, preferred_element_type=jnp.float32).astype(jnp.bfloat16)
        keyed = jnp.dot(encoded, key_weight, preferred_element_type=jnp.float32).astype(jnp.bfloat16)
        valued = jnp.dot(encoded, value_weight, preferred_element_type=jnp.float32).astype(jnp.bfloat16)
        query_heads = query.reshape(TGT, H, DH).astype(jnp.float32)
        key_heads = keyed.reshape(LENC, H, DH).astype(jnp.float32)
        value_heads = valued.reshape(LENC, H, DH).astype(jnp.float32)
        scores = jnp.einsum('thd,lhd->htl', query_heads, key_heads) * scale
        valid = jnp.arange(LENC, dtype=jnp.int32) < enc_len
        scores = jnp.where(valid[None, None, :], scores, -1e+30)
        shifted = jnp.exp(scores - lax.optimization_barrier(jnp.max(scores, axis=-1, keepdims=True)))
        probs = shifted / lax.optimization_barrier(jnp.sum(shifted, axis=-1, keepdims=True))
        probs_low = probs.astype(jnp.bfloat16)
        attended = jnp.einsum('htl,lhd->thd', probs_low.astype(jnp.float32), value_heads).reshape(TGT, D).astype(jnp.bfloat16)
        attn_out = round_sum(grouped(attended, output_weight, N_MP))
        layer_out = (hidden32 + attn_out).astype(jnp.bfloat16)
        keep = (jnp.arange(TGT, dtype=jnp.int32) < dec_len)[:, None]
        masked = jnp.where(keep, upstream, jnp.zeros_like(upstream))
        attended_grad = jnp.dot(masked, output_weight.T, preferred_element_type=jnp.float32).astype(jnp.bfloat16)
        grad_heads = attended_grad.reshape(TGT, H, DH).astype(jnp.float32)
        probs_grad = jnp.einsum('thd,lhd->htl', grad_heads, value_heads)
        scores_grad = (probs * (probs_grad - lax.optimization_barrier(jnp.sum(probs * probs_grad, axis=-1, keepdims=True))) * scale).astype(jnp.bfloat16)
        scores_grad32 = scores_grad.astype(jnp.float32)
        q_grad = jnp.einsum('htl,lhd->thd', scores_grad32, key_heads).reshape(TGT, D).astype(jnp.bfloat16)
        k_grad = jnp.einsum('htl,thd->lhd', scores_grad32, query_heads).reshape(LENC, D).astype(jnp.bfloat16)
        v_grad = jnp.einsum('htl,thd->lhd', probs_low.astype(jnp.float32), grad_heads).reshape(LENC, D).astype(jnp.bfloat16)
        normed_grad = round_sum(grouped(q_grad, query_weight.T, N_MP))
        stat = lax.optimization_barrier(jnp.mean(normed_grad * hidden32, axis=-1, keepdims=True))
        input_grad = (masked.astype(jnp.float32) + inv_rms * normed_grad - hidden32 * inv_rms ** 3 * stat).astype(jnp.bfloat16)
        enc_terms = grouped(k_grad, key_weight.T, N_MP) + grouped(v_grad, value_weight.T, N_MP)
        enc_grad = round_sum(enc_terms).astype(jnp.bfloat16)
        query_term = round_once(jnp.dot(normed.T, q_grad, preferred_element_type=jnp.float32))
        key_term = round_once(jnp.dot(encoded.T, k_grad, preferred_element_type=jnp.float32))
        value_term = round_once(jnp.dot(encoded.T, v_grad, preferred_element_type=jnp.float32))
        output_term = round_once(jnp.dot(attended.T, masked, preferred_element_type=jnp.float32))
        totals = (totals[0] + query_term, totals[1] + key_term, totals[2] + value_term, totals[3] + output_term)
        return (totals, (layer_out, input_grad, enc_grad))
    zeros = jnp.zeros((D, D), jnp.float32)
    totals, stacked = lax.scan(one_seq, (zeros, zeros, zeros, zeros), (dec_input, enc_output, cotangent, enc_lengths, dec_lengths))
    return (stacked[0], stacked[1], stacked[2], totals[0].astype(jnp.bfloat16), totals[1].astype(jnp.bfloat16), totals[2].astype(jnp.bfloat16), totals[3].astype(jnp.bfloat16))
```

```python
import functools

import jax
import jax.numpy as jnp
from jax import lax
from jax.experimental import pallas as pl
from jax.experimental.pallas import tpu as pltpu
from jax.sharding import PartitionSpec as P

DH = 256
MESH = pl.DeviceIdType.MESH
F32 = jnp.float32
BF16 = jnp.bfloat16


def local(
    dec_input,
    enc_output,
    query_weight,
    key_weight,
    value_weight,
    output_weight,
    cotangent,
    enc_lengths,
    dec_lengths,
):
    scale = DH ** (-0.5)
    hidden = lax.all_gather(dec_input, "mp", axis=2, tiled=True)[0]
    query_full, key_full, value_full = (
        lax.all_gather(query_weight, "dp", axis=0, tiled=True),
        lax.all_gather(key_weight, "dp", axis=0, tiled=True),
        lax.all_gather(value_weight, "dp", axis=0, tiled=True),
    )
    output_full = lax.all_gather(output_weight, "dp", axis=1, tiled=True)
    encoded = lax.all_gather(enc_output, "mp", axis=1, tiled=True)[0]
    tokens = hidden.shape[0]
    keys_len = encoded.shape[0]
    width = query_weight.shape[1]
    heads_here = width // DH
    hidden32 = hidden.astype(jnp.float32)
    inv_rms = lax.rsqrt(jnp.mean(hidden32 * hidden32, axis=-1, keepdims=True) + 1e-06)
    normed = (hidden32 * inv_rms).astype(jnp.bfloat16)
    query = jnp.dot(normed, query_full, preferred_element_type=jnp.float32).astype(jnp.bfloat16)
    keyed = jnp.dot(encoded, key_full, preferred_element_type=jnp.float32).astype(jnp.bfloat16)
    valued = jnp.dot(encoded, value_full, preferred_element_type=jnp.float32).astype(jnp.bfloat16)
    query_heads = query.reshape(tokens, heads_here, DH)
    key_heads = keyed.reshape(keys_len, heads_here, DH)
    value_heads = valued.reshape(keys_len, heads_here, DH)
    scores = (
        jnp.einsum("thd,lhd->htl", query_heads, key_heads, preferred_element_type=jnp.float32)
        * scale
    )
    valid = jnp.arange(keys_len, dtype=jnp.int32) < enc_lengths[0]
    scores = jnp.where(valid[None, None, :], scores, -1e30)
    shifted = jnp.exp(scores - jnp.max(scores, axis=-1, keepdims=True))
    probs = shifted / jnp.sum(shifted, axis=-1, keepdims=True)
    probs_low = probs.astype(jnp.bfloat16)
    attended = (
        jnp.einsum("htl,lhd->thd", probs_low, value_heads, preferred_element_type=jnp.float32)
        .reshape(tokens, width)
        .astype(jnp.bfloat16)
    )
    partial_out = jnp.dot(attended, output_full, preferred_element_type=jnp.float32)
    out_share = lax.psum_scatter(
        partial_out.astype(jnp.bfloat16), "mp", scatter_dimension=1, tiled=True
    ).astype(jnp.float32)
    own_input = dec_input[0].astype(jnp.float32)
    layer_out = (own_input + out_share).astype(jnp.bfloat16)[None]
    upstream = lax.all_gather(cotangent, "mp", axis=2, tiled=True)[0]
    keep = (jnp.arange(tokens, dtype=jnp.int32) < dec_lengths[0])[:, None]
    masked = jnp.where(keep, upstream, jnp.zeros_like(upstream))
    own_masked = jnp.where(keep, cotangent[0], jnp.zeros_like(cotangent[0]))
    attended_grad = jnp.dot(masked, output_full.T, preferred_element_type=jnp.float32).astype(
        jnp.bfloat16
    )
    grad_heads = attended_grad.reshape(tokens, heads_here, DH)
    probs_grad = jnp.einsum(
        "thd,lhd->htl", grad_heads, value_heads, preferred_element_type=jnp.float32
    )
    scores_grad = (
        probs * (probs_grad - jnp.sum(probs * probs_grad, axis=-1, keepdims=True)) * scale
    ).astype(jnp.bfloat16)
    q_grad = (
        jnp.einsum("htl,lhd->thd", scores_grad, key_heads, preferred_element_type=jnp.float32)
        .reshape(tokens, width)
        .astype(jnp.bfloat16)
    )
    k_grad = (
        jnp.einsum("htl,thd->lhd", scores_grad, query_heads, preferred_element_type=jnp.float32)
        .reshape(keys_len, width)
        .astype(jnp.bfloat16)
    )
    v_grad = (
        jnp.einsum("htl,thd->lhd", probs_low, grad_heads, preferred_element_type=jnp.float32)
        .reshape(keys_len, width)
        .astype(jnp.bfloat16)
    )
    normed_part = jnp.dot(q_grad, query_full.T, preferred_element_type=jnp.float32)
    feature_width = dec_input.shape[2]
    normed_grad = lax.psum(normed_part.astype(jnp.bfloat16), "mp").astype(jnp.float32)
    stat = jnp.mean(normed_grad * hidden32, axis=-1, keepdims=True)
    full_grad = inv_rms * normed_grad - hidden32 * inv_rms**3 * stat
    start = lax.axis_index("mp") * feature_width
    input_share = lax.dynamic_slice_in_dim(full_grad, start, feature_width, 1)
    input_grad = (own_masked.astype(jnp.float32) + input_share).astype(jnp.bfloat16)[None]
    enc_share = lax.psum_scatter(
        (
            jnp.dot(k_grad, key_full.T, preferred_element_type=jnp.float32)
            + jnp.dot(v_grad, value_full.T, preferred_element_type=jnp.float32)
        ).astype(jnp.bfloat16),
        "mp",
        scatter_dimension=0,
        tiled=True,
    )
    enc_grad = enc_share[None]
    weight_share = lax.psum_scatter(
        jnp.concatenate(
            [
                jnp.dot(normed.T, q_grad, preferred_element_type=jnp.float32),
                jnp.dot(encoded.T, k_grad, preferred_element_type=jnp.float32),
                jnp.dot(encoded.T, v_grad, preferred_element_type=jnp.float32),
                jnp.dot(masked.T, attended, preferred_element_type=jnp.float32),
            ],
            axis=1,
        ).astype(jnp.bfloat16),
        "dp",
        scatter_dimension=0,
        tiled=True,
    ).astype(jnp.float32)
    query_grad = weight_share[:, :width].astype(jnp.bfloat16)
    key_grad = weight_share[:, width : 2 * width].astype(jnp.bfloat16)
    value_grad = weight_share[:, 2 * width : 3 * width].astype(jnp.bfloat16)
    output_grad = weight_share[:, 3 * width :].T.astype(jnp.bfloat16)
    return (layer_out, input_grad, enc_grad, query_grad, key_grad, value_grad, output_grad)


NZ = 4


def place():
    y, m = lax.axis_index("dp"), lax.axis_index("mp")
    z, x, c = m // 4, (m // 2) % 2, m % 2
    peers = {
        "up": (y, m + 4),
        "down": (y, m - 4),
        "y": (1 - y, m),
        "x": (y, m + 2 - 4 * x),
        "c": (y, m + 1 - 2 * c),
    }
    return y, z, x, c, peers


def greet(z, peers):
    barrier = pltpu.get_barrier_semaphore()
    for way in ("y", "x", "c"):
        pl.semaphore_signal(barrier, inc=1, device_id=peers[way], device_id_type=MESH)

    @pl.when(z < NZ - 1)
    def _():
        pl.semaphore_signal(barrier, inc=1, device_id=peers["up"], device_id_type=MESH)

    @pl.when(z > 0)
    def _():
        pl.semaphore_signal(barrier, inc=1, device_id=peers["down"], device_id_type=MESH)

    inner = ((z + 1) // 2) % 2
    pl.semaphore_wait(barrier, 4 + inner)


def when(pred, act):
    if pred is None:
        act()
    else:
        pl.when(pred)(act)


def both(a, b):
    return b if a is None else a if b is None else jnp.logical_and(a, b)


class Sends:
    def __init__(self):
        self.open = []

    def start(self, pred, src, dst, sems, at, peer):
        copy = pltpu.make_async_remote_copy(
            src_ref=src,
            dst_ref=dst,
            send_sem=sems.at[0, at],
            recv_sem=sems.at[1, at],
            device_id=peer,
            device_id_type=MESH,
        )
        when(pred, lambda: copy.start())
        self.open.append((pred, copy))

    def finish(self):
        for pred, copy in self.open:
            when(pred, lambda copy=copy: copy.wait_send())


def arrived(pred, dst, sems, at, peer):
    copy = pltpu.make_async_remote_copy(
        src_ref=dst,
        dst_ref=dst,
        send_sem=sems.at[0, at],
        recv_sem=sems.at[1, at],
        device_id=peer,
        device_id_type=MESH,
    )
    when(pred, lambda: copy.wait_recv())


def feature_block(ref, s, j, x, c):
    return ref.at[s, :, pl.ds(pl.multiple_of(j * 1024 + x * 512 + c * 256, 256), 256)]


def row_block(ref, s, j, x, c):
    return ref.at[s, pl.ds(pl.multiple_of(j * 64 + x * 32 + c * 16, 16), 16), :]


def gather_kernel(dec, enc, cot, gd, ge, gc, *sems):
    y, z, x, c, peers = place()
    sends = Sends()
    local_sems, sems = sems[0], sems[1:]
    tensors = []
    for t, (own, out, rows) in enumerate(((dec, gd, False), (enc, ge, True), (cot, gc, False))):
        up, down, ys, xs, cs = sems[5 * t : 5 * t + 5]
        tensors.append((t, own, out, rows, up, down, ys, xs, cs))

    def held(tensor, zz):
        _, own, out, rows = tensor[:4]
        if rows:
            return [
                (row_block(out, y, zz, x, c), True),
                (row_block(out, 2, zz, x, c), False),
            ]
        other = (zz // 2 + y) % 2
        slot = y + (2 - y) * other
        return [(feature_block(out, slot, zz % 2, x, c), other)]

    def onward(tensor, zz, pred, own=None):
        t, _, out, rows, up, down, ys, xs, cs = tensor
        if rows:
            mine = row_block(out, y, zz, x, c)
            far = row_block(out, 2, zz, x, c)
            src, src_far = (mine, far) if own is None else own
            sends.start(pred, src_far, mine, ys, zz, peers["y"])
            sends.start(pred, src, mine, xs, y * 4 + zz, peers["x"])
            sends.start(pred, src, mine, cs, (y * 4 + zz) * 2 + x, peers["c"])
            return
        other = (zz // 2 + y) % 2
        j = zz % 2
        slot = y + (2 - y) * other
        src = feature_block(out, slot, j, x, c) if own is None else own
        mine = feature_block(out, y, j, x, c)
        sends.start(both(pred, other == 1), src, mine, ys, j, peers["y"])
        near = both(pred, other == 0)
        sends.start(near, src, mine, xs, y * 2 + j, peers["x"])
        sends.start(near, src, mine, cs, (y * 2 + j) * 2 + x, peers["c"])

    greet(z, peers)
    local = []
    for tensor in tensors:
        t, own, out, rows, up, down = tensor[:6]
        views = [view for view, _ in held(tensor, z)]
        if rows:
            half = lambda h: own.at[:, pl.ds(pl.multiple_of(h * 2048, 2048), 2048)]
            srcs = [half(y), half(1 - y)]
        else:
            srcs = [own]
        n = len(views)
        for i, (src, view) in enumerate(zip(srcs, views)):
            sends.start(z < NZ - 1, src, view, up, i, peers["up"])
            sends.start(z > 0, src, view, down, i, peers["down"])
        onward(tensor, z, None, tuple(srcs) if rows else srcs[0])
        for i, (src, view) in enumerate(zip(srcs, views)):
            copy = pltpu.make_async_copy(src, view, local_sems.at[2 * t + i])
            copy.start()
            local.append(copy)
    for k in range(NZ - 1):
        for tensor in tensors:
            t, own, out, rows, up, down = tensor[:6]
            below, above = z - 1 - k, z + 1 + k
            has_below, has_above = below >= 0, above < NZ
            low = jnp.maximum(below, 0)
            high = jnp.minimum(above, NZ - 1)
            for zz, ok, sems_way, way, more in (
                (low, has_below, up, "up", z < NZ - 1),
                (high, has_above, down, "down", z > 0),
            ):
                views = [view for view, _ in held(tensor, zz)]
                n = len(views)
                for i, view in enumerate(views):
                    arrived(ok, view, sems_way, k * n + i, peers["c"])
                    if k + 1 < NZ - 1:
                        sends.start(both(ok, more), view, view, sems_way, (k + 1) * n + i, peers[way])
                onward(tensor, zz, ok)
    for tensor in tensors:
        t, own, out, rows, up, down, ys, xs, cs = tensor
        block = row_block if rows else feature_block
        n = 4 if rows else 2
        for j in range(n):
            view = block(out, 1 - y, j, x, c)
            arrived(None, view, ys, j, peers["y"])
            sends.start(None, view, view, xs, (1 - y) * n + j, peers["x"])
            sends.start(None, view, view, cs, ((1 - y) * n + j) * 2 + x, peers["c"])
    for tensor in tensors:
        t, own, out, rows, up, down, ys, xs, cs = tensor
        block = row_block if rows else feature_block
        n = 4 if rows else 2
        for j in range(n):
            for s in (y, 1 - y):
                view = block(out, s, j, 1 - x, c)
                arrived(None, view, xs, s * n + j, peers["x"])
                sends.start(None, view, view, cs, (s * n + j) * 2 + 1 - x, peers["c"])
    for tensor in tensors:
        t, own, out, rows, up, down, ys, xs, cs = tensor
        block = row_block if rows else feature_block
        n = 4 if rows else 2
        for s in range(2):
            for j in range(n):
                for xx in range(2):
                    arrived(None, block(out, s, j, xx, 1 - c), cs, (s * n + j) * 2 + xx, peers["c"])
    for copy in local:
        copy.wait()
    sends.finish()


def gather(dec, enc, cot):
    vmem = pl.BlockSpec(memory_space=pltpu.VMEM)
    out = jax.ShapeDtypeStruct((3, 256, 2048), BF16)
    sems = [pltpu.SemaphoreType.DMA((6,))]
    for rows in (False, True, False):
        n = 2 if rows else 1
        counts = (3 * n, 3 * n, 2 * n, 4 * n, 8 * n)
        sems += [pltpu.SemaphoreType.DMA((2, count)) for count in counts]
    return pl.pallas_call(
        gather_kernel,
        out_shape=(out, out, out),
        in_specs=[vmem] * 3,
        out_specs=(vmem,) * 3,
        scratch_shapes=sems,
        compiler_params=pltpu.CompilerParams(
            collective_id=0, has_side_effects=True, vmem_limit_bytes=40 * 2**20
        ),
        name="gather_activations",
    )(dec, enc, cot)


def scatter_kernel(po, ng, eg, out_o, out_n, out_e, *scratch):
    y, z, x, c, peers = place()
    sends = Sends()
    tensors = []
    for t, (part, out, rows) in enumerate(((po, out_o, False), (ng, out_n, False), (eg, out_e, True))):
        tensors.append((part, out, rows) + tuple(scratch[15 * t : 15 * t + 15]))

    greet(z, peers)
    for part, out, rows, rc, ax, rx, by, ry, v, su, ru, sd, rd, cs, xs, ys, us, ds in tensors:
        block = row_block if rows else feature_block
        n = 4 if rows else 2
        for xx in (1 - x, x):
            for s in (1 - y, y):
                for j in range(n):
                    at = (s * n + j) * 2 + xx
                    sends.start(None, block(part, s, j, xx, 1 - c), rc.at[at], cs, at, peers["c"])

    def across_x(tensor):
        part, out, rows, rc, ax, rx, by, ry, v, su, ru, sd, rd, cs, xs, ys, us, ds = tensor
        block = row_block if rows else feature_block
        n = 4 if rows else 2
        for s in (1 - y, y):
            for j in range(n):
                at = (s * n + j) * 2 + 1 - x
                arrived(None, rc.at[at], cs, at, peers["c"])
                own = block(part, s, j, 1 - x, c)[...].astype(F32)
                ax[s * n + j] = (own + rc[at].astype(F32)).astype(BF16)
                sends.start(None, ax.at[s * n + j], rx.at[s * n + j], xs, s * n + j, peers["x"])

    def across_y(tensor):
        part, out, rows, rc, ax, rx, by, ry, v, su, ru, sd, rd, cs, xs, ys, us, ds = tensor
        block = row_block if rows else feature_block
        n = 4 if rows else 2
        for s in (1 - y, y):
            for j in range(n):
                at = (s * n + j) * 2 + x
                arrived(None, rc.at[at], cs, at, peers["c"])
                arrived(None, rx.at[s * n + j], xs, s * n + j, peers["x"])
                own = block(part, s, j, x, c)[...].astype(F32)
                total = own + rc[at].astype(F32) + rx[s * n + j].astype(F32)
                if s is not y:
                    by[j] = total.astype(BF16)
                    sends.start(None, by.at[j], ry.at[j], ys, j, peers["y"])
                elif rows:
                    v[j, :, pl.ds(pl.multiple_of(y * 2048, 2048), 2048)] = total
                else:
                    v[2 * y + j] = total

    def along_z(tensor):
        part, out, rows, rc, ax, rx, by, ry, v, su, ru, sd, rd, cs, xs, ys, us, ds = tensor
        n = 4 if rows else 2
        for j in range(n):
            arrived(None, ry.at[j], ys, j, peers["y"])
            if rows:
                v[j, :, pl.ds(pl.multiple_of((1 - y) * 2048, 2048), 2048)] = ry[j].astype(F32)
            else:
                v[2 * (1 - y) + j] = ry[j].astype(F32)
        for k in range(NZ):
            for at, buf, sbuf, sems, way, got, on in (
                (NZ - 1 - k, ru, su, us, "up", (z > 0) & (z <= NZ - 1 - k), z < NZ - 1 - k),
                (k, rd, sd, ds, "down", (z < NZ - 1) & (z >= k), z > k),
            ):
                if not (way == "up" and at == 0) and not (way == "down" and at == NZ - 1):
                    arrived(got, buf.at[at], sems, at, peers["c"])
                    more = got & on

                    @pl.when(more)
                    def _(at=at, buf=buf, sbuf=sbuf):
                        sbuf[at] = (v[at] + buf[at].astype(F32)).astype(BF16)

                    @pl.when(jnp.logical_and(on, jnp.logical_not(got)))
                    def _(at=at, sbuf=sbuf):
                        sbuf[at] = v[at].astype(BF16)

                    sends.start(on, sbuf.at[at], buf.at[at], sems, at, peers[way])
        out[...] = v[z]

        @pl.when(z > 0)
        def _():
            out[...] += ru[z].astype(F32)

        @pl.when(z < NZ - 1)
        def _():
            out[...] += rd[z].astype(F32)

    for tensor in tensors:
        across_x(tensor)
    for i, tensor in enumerate(tensors):
        across_y(tensor)
        if i:
            along_z(tensors[i - 1])
    along_z(tensors[-1])
    sends.finish()


def scatter(po, ng, eg):
    vmem = pl.BlockSpec(memory_space=pltpu.VMEM)
    scratch = []
    for rows in (False, False, True):
        n = 4 if rows else 2
        r, w, wz = (16, 2048, 4096) if rows else (256, 256, 256)
        scratch += [
            pltpu.VMEM((4 * n, r, w), BF16),
            pltpu.VMEM((2 * n, r, w), BF16),
            pltpu.VMEM((2 * n, r, w), BF16),
            pltpu.VMEM((n, r, w), BF16),
            pltpu.VMEM((n, r, w), BF16),
            pltpu.VMEM((NZ, r, wz), F32),
        ]
        scratch += [pltpu.VMEM((NZ, r, wz), BF16)] * 4
        scratch += [pltpu.SemaphoreType.DMA((2, k)) for k in (4 * n, 2 * n, n, NZ, NZ)]
    return pl.pallas_call(
        scatter_kernel,
        out_shape=(
            jax.ShapeDtypeStruct((256, 256), F32),
            jax.ShapeDtypeStruct((256, 256), F32),
            jax.ShapeDtypeStruct((16, 4096), F32),
        ),
        in_specs=[vmem] * 3,
        out_specs=(vmem,) * 3,
        scratch_shapes=scratch,
        compiler_params=pltpu.CompilerParams(
            collective_id=1, has_side_effects=True, vmem_limit_bytes=48 * 2**20
        ),
        name="reduce_scatter",
    )(po, ng, eg)


def dot(a, b, dims):
    return lax.dot_general(a, b, (dims, ((), ())), preferred_element_type=F32)


def swap(a):
    return lax.ppermute(a, "dp", [(0, 1), (1, 0)])


def fast(
    dec_input,
    enc_output,
    query_weight,
    key_weight,
    value_weight,
    output_weight,
    cotangent,
    enc_lengths,
    dec_lengths,
):
    y = lax.axis_index("dp")
    scale = DH ** (-0.5)
    tokens = dec_input.shape[1]
    width = NZ * 4 * dec_input.shape[2]
    half = query_weight.shape[0]
    keep = (jnp.arange(tokens, dtype=jnp.int32) < dec_lengths[0])[:, None]
    own_masked = jnp.where(keep, cotangent[0], jnp.zeros_like(cotangent[0]))
    hidden, encoded, masked = gather(dec_input[0], enc_output[0], own_masked)
    hidden, encoded, masked = (
        hidden[:2].astype(F32),
        encoded[:2].reshape(-1, half),
        masked[:2].reshape(-1, half),
    )
    squares = jnp.sum(hidden * hidden, axis=-1)
    inv_rms = lax.rsqrt((squares + swap(squares)) / width + 1e-06)
    normed = (hidden * inv_rms[:, :, None]).astype(BF16).reshape(-1, half)

    def own(parts):
        return lax.dynamic_index_in_dim(parts, y, 0, keepdims=False)

    def project(left, weight, dims):
        parts = dot(left, weight, dims).reshape(2, -1, weight.shape[1 - dims[1][0]])
        theirs = lax.dynamic_index_in_dim(parts, 1 - y, 0, keepdims=False)
        return (own(parts) + swap(theirs)).astype(BF16)

    down = ((1,), (0,))
    keyed = project(encoded, key_weight, down)
    valued = project(encoded, value_weight, down)
    query = project(normed, query_weight, down)
    attended_grad = project(masked, output_weight, ((1,), (1,)))

    scores = dot(query, keyed, ((1,), (1,))) * scale
    valid = jnp.arange(keyed.shape[0], dtype=jnp.int32) < enc_lengths[0]
    scores = jnp.where(valid[None, :], scores, -1e30)
    shifted = jnp.exp(scores - jnp.max(scores, axis=-1, keepdims=True))
    probs = shifted / jnp.sum(shifted, axis=-1, keepdims=True)
    probs_low = probs.astype(BF16)
    attended = dot(probs_low, valued, down).astype(BF16)
    probs_grad = dot(attended_grad, valued, ((1,), (1,)))
    scores_grad = (
        probs * (probs_grad - jnp.sum(probs * probs_grad, axis=-1, keepdims=True)) * scale
    ).astype(BF16)
    q_grad = dot(scores_grad, keyed, down).astype(BF16)
    k_grad = dot(scores_grad, query, ((0,), (0,))).astype(BF16)
    v_grad = dot(probs_low, attended_grad, ((0,), (0,))).astype(BF16)

    def pair(mine):
        theirs = swap(mine)
        first = jnp.where(y == 0, mine, theirs)
        second = jnp.where(y == 0, theirs, mine)
        return jnp.concatenate([first, second], axis=0)

    v_both, att_both, q_both, k_both = pair(v_grad), pair(attended), pair(q_grad), pair(k_grad)
    part_out = dot(att_both, output_weight, down).astype(BF16).reshape(2, -1, half)
    part_normed = dot(q_both, query_weight, ((1,), (1,))).astype(BF16).reshape(2, -1, half)
    part_enc = (
        dot(k_both, key_weight, ((1,), (1,))) + dot(v_both, value_weight, ((1,), (1,)))
    ).astype(BF16).reshape(2, -1, half)
    stats = lax.psum(jnp.sum(part_normed.astype(F32) * hidden, axis=-1), ("dp", "mp")) / width
    out_sum, normed_grad, enc_sum = scatter(part_out, part_normed, part_enc)

    rows = ((0,), (0,))
    query_grad = dot(normed, q_both, rows).astype(BF16)
    key_grad = dot(encoded, k_both, rows).astype(BF16)
    value_grad = dot(encoded, v_both, rows).astype(BF16)
    output_grad = dot(att_both, masked, rows).astype(BF16)

    own_input = dec_input[0].astype(F32)
    layer_out = (own_input + out_sum).astype(BF16)[None]
    inv, stat = own(inv_rms)[:, None], own(stats)[:, None]
    input_grad = (
        own_masked.astype(F32) + inv * normed_grad - own_input * inv**3 * stat
    ).astype(BF16)[None]
    enc_grad = enc_sum.astype(BF16)[None]
    return (layer_out, input_grad, enc_grad, query_grad, key_grad, value_grad, output_grad)


def solution(mesh):
    in_specs = (
        P("dp", None, "mp"),
        P("dp", "mp", None),
        P("dp", "mp"),
        P("dp", "mp"),
        P("dp", "mp"),
        P("mp", "dp"),
        P("dp", None, "mp"),
        P("dp"),
        P("dp"),
    )
    out_specs = (
        P("dp", None, "mp"),
        P("dp", None, "mp"),
        P("dp", "mp", None),
        P("dp", "mp"),
        P("dp", "mp"),
        P("dp", "mp"),
        P("mp", "dp"),
    )
    program = fast if dict(mesh.shape) == {"dp": 2, "mp": 16} else local
    return jax.shard_map(program, mesh=mesh, in_specs=in_specs, out_specs=out_specs, check_vma=False)
```

```python
import functools

import jax
import jax.numpy as jnp
from jax import lax
from jax.experimental import pallas as pl
from jax.experimental.pallas import tpu as pltpu
from jax.sharding import PartitionSpec as P

DH = 256
MESH = pl.DeviceIdType.MESH
F32 = jnp.float32
BF16 = jnp.bfloat16


def local(
    dec_input,
    enc_output,
    query_weight,
    key_weight,
    value_weight,
    output_weight,
    cotangent,
    enc_lengths,
    dec_lengths,
):
    scale = DH ** (-0.5)
    hidden = lax.all_gather(dec_input, "mp", axis=2, tiled=True)[0]
    query_full, key_full, value_full = (
        lax.all_gather(query_weight, "dp", axis=0, tiled=True),
        lax.all_gather(key_weight, "dp", axis=0, tiled=True),
        lax.all_gather(value_weight, "dp", axis=0, tiled=True),
    )
    output_full = lax.all_gather(output_weight, "dp", axis=1, tiled=True)
    encoded = lax.all_gather(enc_output, "mp", axis=1, tiled=True)[0]
    tokens = hidden.shape[0]
    keys_len = encoded.shape[0]
    width = query_weight.shape[1]
    heads_here = width // DH
    hidden32 = hidden.astype(jnp.float32)
    inv_rms = lax.rsqrt(jnp.mean(hidden32 * hidden32, axis=-1, keepdims=True) + 1e-06)
    normed = (hidden32 * inv_rms).astype(jnp.bfloat16)
    query = jnp.dot(normed, query_full, preferred_element_type=jnp.float32).astype(jnp.bfloat16)
    keyed = jnp.dot(encoded, key_full, preferred_element_type=jnp.float32).astype(jnp.bfloat16)
    valued = jnp.dot(encoded, value_full, preferred_element_type=jnp.float32).astype(jnp.bfloat16)
    query_heads = query.reshape(tokens, heads_here, DH)
    key_heads = keyed.reshape(keys_len, heads_here, DH)
    value_heads = valued.reshape(keys_len, heads_here, DH)
    scores = (
        jnp.einsum("thd,lhd->htl", query_heads, key_heads, preferred_element_type=jnp.float32)
        * scale
    )
    valid = jnp.arange(keys_len, dtype=jnp.int32) < enc_lengths[0]
    scores = jnp.where(valid[None, None, :], scores, -1e30)
    shifted = jnp.exp(scores - jnp.max(scores, axis=-1, keepdims=True))
    probs = shifted / jnp.sum(shifted, axis=-1, keepdims=True)
    probs_low = probs.astype(jnp.bfloat16)
    attended = (
        jnp.einsum("htl,lhd->thd", probs_low, value_heads, preferred_element_type=jnp.float32)
        .reshape(tokens, width)
        .astype(jnp.bfloat16)
    )
    partial_out = jnp.dot(attended, output_full, preferred_element_type=jnp.float32)
    out_share = lax.psum_scatter(
        partial_out.astype(jnp.bfloat16), "mp", scatter_dimension=1, tiled=True
    ).astype(jnp.float32)
    own_input = dec_input[0].astype(jnp.float32)
    layer_out = (own_input + out_share).astype(jnp.bfloat16)[None]
    upstream = lax.all_gather(cotangent, "mp", axis=2, tiled=True)[0]
    keep = (jnp.arange(tokens, dtype=jnp.int32) < dec_lengths[0])[:, None]
    masked = jnp.where(keep, upstream, jnp.zeros_like(upstream))
    own_masked = jnp.where(keep, cotangent[0], jnp.zeros_like(cotangent[0]))
    attended_grad = jnp.dot(masked, output_full.T, preferred_element_type=jnp.float32).astype(
        jnp.bfloat16
    )
    grad_heads = attended_grad.reshape(tokens, heads_here, DH)
    probs_grad = jnp.einsum(
        "thd,lhd->htl", grad_heads, value_heads, preferred_element_type=jnp.float32
    )
    scores_grad = (
        probs * (probs_grad - jnp.sum(probs * probs_grad, axis=-1, keepdims=True)) * scale
    ).astype(jnp.bfloat16)
    q_grad = (
        jnp.einsum("htl,lhd->thd", scores_grad, key_heads, preferred_element_type=jnp.float32)
        .reshape(tokens, width)
        .astype(jnp.bfloat16)
    )
    k_grad = (
        jnp.einsum("htl,thd->lhd", scores_grad, query_heads, preferred_element_type=jnp.float32)
        .reshape(keys_len, width)
        .astype(jnp.bfloat16)
    )
    v_grad = (
        jnp.einsum("htl,thd->lhd", probs_low, grad_heads, preferred_element_type=jnp.float32)
        .reshape(keys_len, width)
        .astype(jnp.bfloat16)
    )
    normed_part = jnp.dot(q_grad, query_full.T, preferred_element_type=jnp.float32)
    feature_width = dec_input.shape[2]
    normed_grad = lax.psum(normed_part.astype(jnp.bfloat16), "mp").astype(jnp.float32)
    stat = jnp.mean(normed_grad * hidden32, axis=-1, keepdims=True)
    full_grad = inv_rms * normed_grad - hidden32 * inv_rms**3 * stat
    start = lax.axis_index("mp") * feature_width
    input_share = lax.dynamic_slice_in_dim(full_grad, start, feature_width, 1)
    input_grad = (own_masked.astype(jnp.float32) + input_share).astype(jnp.bfloat16)[None]
    enc_share = lax.psum_scatter(
        (
            jnp.dot(k_grad, key_full.T, preferred_element_type=jnp.float32)
            + jnp.dot(v_grad, value_full.T, preferred_element_type=jnp.float32)
        ).astype(jnp.bfloat16),
        "mp",
        scatter_dimension=0,
        tiled=True,
    )
    enc_grad = enc_share[None]
    weight_share = lax.psum_scatter(
        jnp.concatenate(
            [
                jnp.dot(normed.T, q_grad, preferred_element_type=jnp.float32),
                jnp.dot(encoded.T, k_grad, preferred_element_type=jnp.float32),
                jnp.dot(encoded.T, v_grad, preferred_element_type=jnp.float32),
                jnp.dot(masked.T, attended, preferred_element_type=jnp.float32),
            ],
            axis=1,
        ).astype(jnp.bfloat16),
        "dp",
        scatter_dimension=0,
        tiled=True,
    ).astype(jnp.float32)
    query_grad = weight_share[:, :width].astype(jnp.bfloat16)
    key_grad = weight_share[:, width : 2 * width].astype(jnp.bfloat16)
    value_grad = weight_share[:, 2 * width : 3 * width].astype(jnp.bfloat16)
    output_grad = weight_share[:, 3 * width :].T.astype(jnp.bfloat16)
    return (layer_out, input_grad, enc_grad, query_grad, key_grad, value_grad, output_grad)


NZ = 4


def place():
    y, m = lax.axis_index("dp"), lax.axis_index("mp")
    z, x, c = m // 4, (m // 2) % 2, m % 2
    peers = {
        "up": (y, m + 4),
        "down": (y, m - 4),
        "y": (1 - y, m),
        "x": (y, m + 2 - 4 * x),
        "c": (y, m + 1 - 2 * c),
    }
    return y, z, x, c, peers


def greet(z, peers):
    barrier = pltpu.get_barrier_semaphore()
    for way in ("y", "x", "c"):
        pl.semaphore_signal(barrier, inc=1, device_id=peers[way], device_id_type=MESH)

    @pl.when(z < NZ - 1)
    def _():
        pl.semaphore_signal(barrier, inc=1, device_id=peers["up"], device_id_type=MESH)

    @pl.when(z > 0)
    def _():
        pl.semaphore_signal(barrier, inc=1, device_id=peers["down"], device_id_type=MESH)

    inner = ((z + 1) // 2) % 2
    pl.semaphore_wait(barrier, 4 + inner)


def when(pred, act):
    if pred is None:
        act()
    else:
        pl.when(pred)(act)


def both(a, b):
    return b if a is None else a if b is None else jnp.logical_and(a, b)


class Sends:
    def __init__(self):
        self.open = []

    def start(self, pred, src, dst, sems, at, peer):
        copy = pltpu.make_async_remote_copy(
            src_ref=src,
            dst_ref=dst,
            send_sem=sems.at[0, at],
            recv_sem=sems.at[1, at],
            device_id=peer,
            device_id_type=MESH,
        )
        when(pred, lambda: copy.start())
        self.open.append((pred, copy))

    def finish(self):
        for pred, copy in self.open:
            when(pred, lambda copy=copy: copy.wait_send())


def arrived(pred, dst, sems, at, peer):
    copy = pltpu.make_async_remote_copy(
        src_ref=dst,
        dst_ref=dst,
        send_sem=sems.at[0, at],
        recv_sem=sems.at[1, at],
        device_id=peer,
        device_id_type=MESH,
    )
    when(pred, lambda: copy.wait_recv())


def feature_block(ref, s, j, x, c):
    return ref.at[s, :, pl.ds(pl.multiple_of(j * 1024 + x * 512 + c * 256, 256), 256)]


def row_block(ref, s, j, x, c):
    return ref.at[s, pl.ds(pl.multiple_of(j * 64 + x * 32 + c * 16, 16), 16), :]


def gather_kernel(dec, enc, cot, gd, ge, gc, *sems):
    y, z, x, c, peers = place()
    sends = Sends()
    local_sems, sems = sems[0], sems[1:]
    tensors = []
    for t, (own, out, rows) in enumerate(((dec, gd, False), (enc, ge, True), (cot, gc, False))):
        up, down, ys, xs, cs = sems[5 * t : 5 * t + 5]
        tensors.append((t, own, out, rows, up, down, ys, xs, cs))

    def held(tensor, zz):
        _, own, out, rows = tensor[:4]
        if rows:
            return [
                (row_block(out, y, zz, x, c), True),
                (row_block(out, 2, zz, x, c), False),
            ]
        other = (zz // 2 + y) % 2
        slot = y + (2 - y) * other
        return [(feature_block(out, slot, zz % 2, x, c), other)]

    def onward(tensor, zz, pred, own=None):
        t, _, out, rows, up, down, ys, xs, cs = tensor
        if rows:
            mine = row_block(out, y, zz, x, c)
            far = row_block(out, 2, zz, x, c)
            src, src_far = (mine, far) if own is None else own
            sends.start(pred, src_far, mine, ys, zz, peers["y"])
            sends.start(pred, src, mine, xs, y * 4 + zz, peers["x"])
            sends.start(pred, src, mine, cs, (y * 4 + zz) * 2 + x, peers["c"])
            return
        other = (zz // 2 + y) % 2
        j = zz % 2
        slot = y + (2 - y) * other
        src = feature_block(out, slot, j, x, c) if own is None else own
        mine = feature_block(out, y, j, x, c)
        sends.start(both(pred, other == 1), src, mine, ys, j, peers["y"])
        near = both(pred, other == 0)
        sends.start(near, src, mine, xs, y * 2 + j, peers["x"])
        sends.start(near, src, mine, cs, (y * 2 + j) * 2 + x, peers["c"])

    greet(z, peers)
    local = []
    for tensor in tensors:
        t, own, out, rows, up, down = tensor[:6]
        views = [view for view, _ in held(tensor, z)]
        if rows:
            half = lambda h: own.at[:, pl.ds(pl.multiple_of(h * 2048, 2048), 2048)]
            srcs = [half(y), half(1 - y)]
        else:
            srcs = [own]
        n = len(views)
        for i, (src, view) in enumerate(zip(srcs, views)):
            sends.start(z < NZ - 1, src, view, up, i, peers["up"])
            sends.start(z > 0, src, view, down, i, peers["down"])
        onward(tensor, z, None, tuple(srcs) if rows else srcs[0])
        for i, (src, view) in enumerate(zip(srcs, views)):
            copy = pltpu.make_async_copy(src, view, local_sems.at[2 * t + i])
            copy.start()
            local.append(copy)
    for k in range(NZ - 1):
        for tensor in tensors:
            t, own, out, rows, up, down = tensor[:6]
            below, above = z - 1 - k, z + 1 + k
            has_below, has_above = below >= 0, above < NZ
            low = jnp.maximum(below, 0)
            high = jnp.minimum(above, NZ - 1)
            for zz, ok, sems_way, way, more in (
                (low, has_below, up, "up", z < NZ - 1),
                (high, has_above, down, "down", z > 0),
            ):
                views = [view for view, _ in held(tensor, zz)]
                n = len(views)
                for i, view in enumerate(views):
                    arrived(ok, view, sems_way, k * n + i, peers["c"])
                    if k + 1 < NZ - 1:
                        sends.start(both(ok, more), view, view, sems_way, (k + 1) * n + i, peers[way])
                onward(tensor, zz, ok)
    for tensor in tensors:
        t, own, out, rows, up, down, ys, xs, cs = tensor
        block = row_block if rows else feature_block
        n = 4 if rows else 2
        for j in range(n):
            view = block(out, 1 - y, j, x, c)
            arrived(None, view, ys, j, peers["y"])
            sends.start(None, view, view, xs, (1 - y) * n + j, peers["x"])
            sends.start(None, view, view, cs, ((1 - y) * n + j) * 2 + x, peers["c"])
    for tensor in tensors:
        t, own, out, rows, up, down, ys, xs, cs = tensor
        block = row_block if rows else feature_block
        n = 4 if rows else 2
        for j in range(n):
            for s in (y, 1 - y):
                view = block(out, s, j, 1 - x, c)
                arrived(None, view, xs, s * n + j, peers["x"])
                sends.start(None, view, view, cs, (s * n + j) * 2 + 1 - x, peers["c"])
    for tensor in tensors:
        t, own, out, rows, up, down, ys, xs, cs = tensor
        block = row_block if rows else feature_block
        n = 4 if rows else 2
        for s in range(2):
            for j in range(n):
                for xx in range(2):
                    arrived(None, block(out, s, j, xx, 1 - c), cs, (s * n + j) * 2 + xx, peers["c"])
    for copy in local:
        copy.wait()
    sends.finish()


def gather(dec, enc, cot):
    vmem = pl.BlockSpec(memory_space=pltpu.VMEM)
    out = jax.ShapeDtypeStruct((3, 256, 2048), BF16)
    sems = [pltpu.SemaphoreType.DMA((6,))]
    for rows in (False, True, False):
        n = 2 if rows else 1
        counts = (3 * n, 3 * n, 2 * n, 4 * n, 8 * n)
        sems += [pltpu.SemaphoreType.DMA((2, count)) for count in counts]
    return pl.pallas_call(
        gather_kernel,
        out_shape=(out, out, out),
        in_specs=[vmem] * 3,
        out_specs=(vmem,) * 3,
        scratch_shapes=sems,
        compiler_params=pltpu.CompilerParams(
            collective_id=0, has_side_effects=True, vmem_limit_bytes=40 * 2**20
        ),
        name="gather_activations",
    )(dec, enc, cot)


def line_peer(y, z, x, c, d):
    return (y, ((z + d) % NZ) * 4 + x * 2 + c)


def greet_all(place_here, peers):
    barrier = pltpu.get_barrier_semaphore()
    targets = [peers[way] for way in ("y", "x", "c")]
    targets += [line_peer(*place_here, d) for d in range(1, NZ)]
    for target in targets:
        pl.semaphore_signal(barrier, inc=1, device_id=target, device_id_type=MESH)
    pl.semaphore_wait(barrier, len(targets))


def scatter_kernel(po, ng, eg, stat, out_o, out_n, out_e, out_s, *scratch):
    y, z, x, c, peers = place()
    here = (y, z, x, c)
    sends = Sends()
    stat_got, stat_sum, stat_sems = scratch[:3]
    scratch = scratch[3:]
    tensors = []
    for t, (part, out, rows) in enumerate(((po, out_o, False), (ng, out_n, False), (eg, out_e, True))):
        tensors.append((part, out, rows) + tuple(scratch[12 * t : 12 * t + 12]))

    greet_all(here, peers)
    sends.start(None, stat, stat_got.at[0], stat_sems, 0, peers["c"])
    for part, out, rows, rc, ax, rx, by, ry, v, sz, rz, cs, xs, ys, zs in tensors:
        block = row_block if rows else feature_block
        n = 4 if rows else 2
        for xx in (1 - x, x):
            for s in (1 - y, y):
                for j in range(n):
                    at = (s * n + j) * 2 + xx
                    sends.start(None, block(part, s, j, xx, 1 - c), rc.at[at], cs, at, peers["c"])

    def across_x(tensor):
        part, out, rows, rc, ax, rx, by, ry, v, sz, rz, cs, xs, ys, zs = tensor
        block = row_block if rows else feature_block
        n = 4 if rows else 2
        for s in (1 - y, y):
            for j in range(n):
                at = (s * n + j) * 2 + 1 - x
                arrived(None, rc.at[at], cs, at, peers["c"])
                own = block(part, s, j, 1 - x, c)[...].astype(F32)
                ax[s * n + j] = (own + rc[at].astype(F32)).astype(BF16)
                sends.start(None, ax.at[s * n + j], rx.at[s * n + j], xs, s * n + j, peers["x"])

    def across_y(tensor):
        part, out, rows, rc, ax, rx, by, ry, v, sz, rz, cs, xs, ys, zs = tensor
        block = row_block if rows else feature_block
        n = 4 if rows else 2
        for theirs in (True, False):
            s = 1 - y if theirs else y
            for j in range(n):
                at = (s * n + j) * 2 + x
                arrived(None, rc.at[at], cs, at, peers["c"])
                arrived(None, rx.at[s * n + j], xs, s * n + j, peers["x"])
                own = block(part, s, j, x, c)[...].astype(F32)
                total = own + rc[at].astype(F32) + rx[s * n + j].astype(F32)
                if theirs:
                    by[j] = total.astype(BF16)
                    sends.start(None, by.at[j], ry.at[j], ys, j, peers["y"])
                elif rows:
                    v[j, :, pl.ds(pl.multiple_of(y * 2048, 2048), 2048)] = total
                else:
                    v[2 * y + j] = total

    def along_z(tensor):
        part, out, rows, rc, ax, rx, by, ry, v, sz, rz, cs, xs, ys, zs = tensor
        n = 4 if rows else 2
        for j in range(n):
            arrived(None, ry.at[j], ys, j, peers["y"])
            if rows:
                v[j, :, pl.ds(pl.multiple_of((1 - y) * 2048, 2048), 2048)] = ry[j].astype(F32)
            else:
                v[2 * (1 - y) + j] = ry[j].astype(F32)
        for d in (2, 1, 3):
            sz[d - 1] = v[(z + d) % NZ].astype(BF16)
            sends.start(None, sz.at[d - 1], rz.at[d - 1], zs, d - 1, line_peer(*here, d))

    def close(tensor):
        part, out, rows, rc, ax, rx, by, ry, v, sz, rz, cs, xs, ys, zs = tensor
        total = v[z]
        for d in range(1, NZ):
            arrived(None, rz.at[d - 1], zs, d - 1, peers["c"])
            total += rz[d - 1].astype(F32)
        out[...] = total

    def stat_step(k, way):
        arrived(None, stat_got.at[k], stat_sems, k, peers["c"])
        held = stat[...] if k == 0 else stat_sum[k - 1]
        stat_sum[k] = held + stat_got[k]
        if way:
            sends.start(None, stat_sum.at[k], stat_got.at[k + 1], stat_sems, k + 1, peers[way])

    across_x(tensors[0])
    stat_step(0, "x")
    across_x(tensors[1])
    across_x(tensors[2])
    stat_step(1, "y")
    across_y(tensors[0])
    across_y(tensors[1])
    stat_step(2, None)
    for d in range(1, NZ):
        sends.start(
            None, stat_sum.at[2], stat_got.at[2 + d], stat_sems, 2 + d, line_peer(*here, d)
        )
    along_z(tensors[0])
    across_y(tensors[2])
    along_z(tensors[1])
    along_z(tensors[2])
    total = stat_sum[2]
    for d in range(1, NZ):
        arrived(None, stat_got.at[2 + d], stat_sems, 2 + d, peers["c"])
        total += stat_got[2 + d]
    out_s[...] = total
    for tensor in tensors:
        close(tensor)
    sends.finish()


def scatter(po, ng, eg, stat):
    vmem = pl.BlockSpec(memory_space=pltpu.VMEM)
    scratch = [
        pltpu.VMEM((6, 8, 128), F32),
        pltpu.VMEM((3, 8, 128), F32),
        pltpu.SemaphoreType.DMA((2, 6)),
    ]
    for rows in (False, False, True):
        n = 4 if rows else 2
        r, w, wz = (16, 2048, 4096) if rows else (256, 256, 256)
        scratch += [
            pltpu.VMEM((4 * n, r, w), BF16),
            pltpu.VMEM((2 * n, r, w), BF16),
            pltpu.VMEM((2 * n, r, w), BF16),
            pltpu.VMEM((n, r, w), BF16),
            pltpu.VMEM((n, r, w), BF16),
            pltpu.VMEM((NZ, r, wz), F32),
        ]
        scratch += [pltpu.VMEM((NZ - 1, r, wz), BF16)] * 2
        scratch += [pltpu.SemaphoreType.DMA((2, k)) for k in (4 * n, 2 * n, n, NZ - 1)]
    return pl.pallas_call(
        scatter_kernel,
        out_shape=(
            jax.ShapeDtypeStruct((256, 256), F32),
            jax.ShapeDtypeStruct((256, 256), F32),
            jax.ShapeDtypeStruct((16, 4096), F32),
            jax.ShapeDtypeStruct((8, 128), F32),
        ),
        in_specs=[vmem] * 4,
        out_specs=(vmem,) * 4,
        scratch_shapes=scratch,
        compiler_params=pltpu.CompilerParams(
            collective_id=1, has_side_effects=True, vmem_limit_bytes=48 * 2**20
        ),
        name="reduce_scatter",
    )(po, ng, eg, stat)


def dot(a, b, dims):
    return lax.dot_general(a, b, (dims, ((), ())), preferred_element_type=F32)


def swap(a):
    return lax.ppermute(a, "dp", [(0, 1), (1, 0)])


def fast(
    dec_input,
    enc_output,
    query_weight,
    key_weight,
    value_weight,
    output_weight,
    cotangent,
    enc_lengths,
    dec_lengths,
):
    y = lax.axis_index("dp")
    scale = DH ** (-0.5)
    tokens = dec_input.shape[1]
    width = NZ * 4 * dec_input.shape[2]
    half = query_weight.shape[0]
    keep = (jnp.arange(tokens, dtype=jnp.int32) < dec_lengths[0])[:, None]
    own_masked = jnp.where(keep, cotangent[0], jnp.zeros_like(cotangent[0]))
    hidden, encoded, masked = gather(dec_input[0], enc_output[0], own_masked)
    hidden, encoded, masked = (
        hidden[:2].astype(F32),
        encoded[:2].reshape(-1, half),
        masked[:2].reshape(-1, half),
    )
    squares = jnp.sum(hidden * hidden, axis=-1)
    inv_rms = lax.rsqrt((squares + swap(squares)) / width + 1e-06)
    normed = (hidden * inv_rms[:, :, None]).astype(BF16).reshape(-1, half)

    def own(parts):
        return lax.dynamic_index_in_dim(parts, y, 0, keepdims=False)

    def project(left, weight, dims):
        parts = dot(left, weight, dims).reshape(2, -1, weight.shape[1 - dims[1][0]])
        theirs = lax.dynamic_index_in_dim(parts, 1 - y, 0, keepdims=False)
        return (own(parts) + swap(theirs)).astype(BF16)

    down = ((1,), (0,))
    keyed = project(encoded, key_weight, down)
    valued = project(encoded, value_weight, down)
    query = project(normed, query_weight, down)
    attended_grad = project(masked, output_weight, ((1,), (1,)))

    scores = dot(query, keyed, ((1,), (1,))) * scale
    valid = jnp.arange(keyed.shape[0], dtype=jnp.int32) < enc_lengths[0]
    scores = jnp.where(valid[None, :], scores, -1e30)
    shifted = jnp.exp(scores - jnp.max(scores, axis=-1, keepdims=True))
    probs = shifted / jnp.sum(shifted, axis=-1, keepdims=True)
    probs_low = probs.astype(BF16)
    attended = dot(probs_low, valued, down).astype(BF16)
    probs_grad = dot(attended_grad, valued, ((1,), (1,)))
    scores_grad = (
        probs * (probs_grad - jnp.sum(probs * probs_grad, axis=-1, keepdims=True)) * scale
    ).astype(BF16)
    q_grad = dot(scores_grad, keyed, down).astype(BF16)
    k_grad = dot(scores_grad, query, ((0,), (0,))).astype(BF16)
    v_grad = dot(probs_low, attended_grad, ((0,), (0,))).astype(BF16)

    def pair(mine):
        theirs = swap(mine)
        first = jnp.where(y == 0, mine, theirs)
        second = jnp.where(y == 0, theirs, mine)
        return jnp.concatenate([first, second], axis=0)

    v_both, att_both, q_both, k_both = pair(v_grad), pair(attended), pair(q_grad), pair(k_grad)
    part_out = dot(att_both, output_weight, down).astype(BF16).reshape(2, -1, half)
    part_normed = dot(q_both, query_weight, ((1,), (1,))).astype(BF16).reshape(2, -1, half)
    part_enc = (
        dot(k_both, key_weight, ((1,), (1,))) + dot(v_both, value_weight, ((1,), (1,)))
    ).astype(BF16).reshape(2, -1, half)
    stats = jnp.sum(part_normed.astype(F32) * hidden, axis=-1).reshape(4, 128)
    stats = jnp.concatenate([stats, jnp.zeros_like(stats)], axis=0)
    out_sum, normed_grad, enc_sum, stats = scatter(part_out, part_normed, part_enc, stats)
    stats = stats[:4].reshape(2, tokens) / width

    rows = ((0,), (0,))
    query_grad = dot(normed, q_both, rows).astype(BF16)
    key_grad = dot(encoded, k_both, rows).astype(BF16)
    value_grad = dot(encoded, v_both, rows).astype(BF16)
    output_grad = dot(att_both, masked, rows).astype(BF16)

    own_input = dec_input[0].astype(F32)
    layer_out = (own_input + out_sum).astype(BF16)[None]
    inv, stat = own(inv_rms)[:, None], own(stats)[:, None]
    input_grad = (
        own_masked.astype(F32) + inv * normed_grad - own_input * inv**3 * stat
    ).astype(BF16)[None]
    enc_grad = enc_sum.astype(BF16)[None]
    return (layer_out, input_grad, enc_grad, query_grad, key_grad, value_grad, output_grad)


def solution(mesh):
    in_specs = (
        P("dp", None, "mp"),
        P("dp", "mp", None),
        P("dp", "mp"),
        P("dp", "mp"),
        P("dp", "mp"),
        P("mp", "dp"),
        P("dp", None, "mp"),
        P("dp"),
        P("dp"),
    )
    out_specs = (
        P("dp", None, "mp"),
        P("dp", None, "mp"),
        P("dp", "mp", None),
        P("dp", "mp"),
        P("dp", "mp"),
        P("dp", "mp"),
        P("mp", "dp"),
    )
    program = fast if dict(mesh.shape) == {"dp": 2, "mp": 16} else local
    return jax.shard_map(program, mesh=mesh, in_specs=in_specs, out_specs=out_specs, check_vma=False)
```

```python
import functools

import jax
import jax.numpy as jnp
from jax import lax
from jax.experimental import pallas as pl
from jax.experimental.pallas import tpu as pltpu
from jax.sharding import PartitionSpec as P

DH = 256
MESH = pl.DeviceIdType.MESH
F32 = jnp.float32
BF16 = jnp.bfloat16


def local(
    dec_input,
    enc_output,
    query_weight,
    key_weight,
    value_weight,
    output_weight,
    cotangent,
    enc_lengths,
    dec_lengths,
):
    scale = DH ** (-0.5)
    hidden = lax.all_gather(dec_input, "mp", axis=2, tiled=True)[0]
    query_full, key_full, value_full = (
        lax.all_gather(query_weight, "dp", axis=0, tiled=True),
        lax.all_gather(key_weight, "dp", axis=0, tiled=True),
        lax.all_gather(value_weight, "dp", axis=0, tiled=True),
    )
    output_full = lax.all_gather(output_weight, "dp", axis=1, tiled=True)
    encoded = lax.all_gather(enc_output, "mp", axis=1, tiled=True)[0]
    tokens = hidden.shape[0]
    keys_len = encoded.shape[0]
    width = query_weight.shape[1]
    heads_here = width // DH
    hidden32 = hidden.astype(jnp.float32)
    inv_rms = lax.rsqrt(jnp.mean(hidden32 * hidden32, axis=-1, keepdims=True) + 1e-06)
    normed = (hidden32 * inv_rms).astype(jnp.bfloat16)
    query = jnp.dot(normed, query_full, preferred_element_type=jnp.float32).astype(jnp.bfloat16)
    keyed = jnp.dot(encoded, key_full, preferred_element_type=jnp.float32).astype(jnp.bfloat16)
    valued = jnp.dot(encoded, value_full, preferred_element_type=jnp.float32).astype(jnp.bfloat16)
    query_heads = query.reshape(tokens, heads_here, DH)
    key_heads = keyed.reshape(keys_len, heads_here, DH)
    value_heads = valued.reshape(keys_len, heads_here, DH)
    scores = (
        jnp.einsum("thd,lhd->htl", query_heads, key_heads, preferred_element_type=jnp.float32)
        * scale
    )
    valid = jnp.arange(keys_len, dtype=jnp.int32) < enc_lengths[0]
    scores = jnp.where(valid[None, None, :], scores, -1e30)
    shifted = jnp.exp(scores - jnp.max(scores, axis=-1, keepdims=True))
    probs = shifted / jnp.sum(shifted, axis=-1, keepdims=True)
    probs_low = probs.astype(jnp.bfloat16)
    attended = (
        jnp.einsum("htl,lhd->thd", probs_low, value_heads, preferred_element_type=jnp.float32)
        .reshape(tokens, width)
        .astype(jnp.bfloat16)
    )
    partial_out = jnp.dot(attended, output_full, preferred_element_type=jnp.float32)
    out_share = lax.psum_scatter(
        partial_out.astype(jnp.bfloat16), "mp", scatter_dimension=1, tiled=True
    ).astype(jnp.float32)
    own_input = dec_input[0].astype(jnp.float32)
    layer_out = (own_input + out_share).astype(jnp.bfloat16)[None]
    upstream = lax.all_gather(cotangent, "mp", axis=2, tiled=True)[0]
    keep = (jnp.arange(tokens, dtype=jnp.int32) < dec_lengths[0])[:, None]
    masked = jnp.where(keep, upstream, jnp.zeros_like(upstream))
    own_masked = jnp.where(keep, cotangent[0], jnp.zeros_like(cotangent[0]))
    attended_grad = jnp.dot(masked, output_full.T, preferred_element_type=jnp.float32).astype(
        jnp.bfloat16
    )
    grad_heads = attended_grad.reshape(tokens, heads_here, DH)
    probs_grad = jnp.einsum(
        "thd,lhd->htl", grad_heads, value_heads, preferred_element_type=jnp.float32
    )
    scores_grad = (
        probs * (probs_grad - jnp.sum(probs * probs_grad, axis=-1, keepdims=True)) * scale
    ).astype(jnp.bfloat16)
    q_grad = (
        jnp.einsum("htl,lhd->thd", scores_grad, key_heads, preferred_element_type=jnp.float32)
        .reshape(tokens, width)
        .astype(jnp.bfloat16)
    )
    k_grad = (
        jnp.einsum("htl,thd->lhd", scores_grad, query_heads, preferred_element_type=jnp.float32)
        .reshape(keys_len, width)
        .astype(jnp.bfloat16)
    )
    v_grad = (
        jnp.einsum("htl,thd->lhd", probs_low, grad_heads, preferred_element_type=jnp.float32)
        .reshape(keys_len, width)
        .astype(jnp.bfloat16)
    )
    normed_part = jnp.dot(q_grad, query_full.T, preferred_element_type=jnp.float32)
    feature_width = dec_input.shape[2]
    normed_grad = lax.psum(normed_part.astype(jnp.bfloat16), "mp").astype(jnp.float32)
    stat = jnp.mean(normed_grad * hidden32, axis=-1, keepdims=True)
    full_grad = inv_rms * normed_grad - hidden32 * inv_rms**3 * stat
    start = lax.axis_index("mp") * feature_width
    input_share = lax.dynamic_slice_in_dim(full_grad, start, feature_width, 1)
    input_grad = (own_masked.astype(jnp.float32) + input_share).astype(jnp.bfloat16)[None]
    enc_share = lax.psum_scatter(
        (
            jnp.dot(k_grad, key_full.T, preferred_element_type=jnp.float32)
            + jnp.dot(v_grad, value_full.T, preferred_element_type=jnp.float32)
        ).astype(jnp.bfloat16),
        "mp",
        scatter_dimension=0,
        tiled=True,
    )
    enc_grad = enc_share[None]
    weight_share = lax.psum_scatter(
        jnp.concatenate(
            [
                jnp.dot(normed.T, q_grad, preferred_element_type=jnp.float32),
                jnp.dot(encoded.T, k_grad, preferred_element_type=jnp.float32),
                jnp.dot(encoded.T, v_grad, preferred_element_type=jnp.float32),
                jnp.dot(masked.T, attended, preferred_element_type=jnp.float32),
            ],
            axis=1,
        ).astype(jnp.bfloat16),
        "dp",
        scatter_dimension=0,
        tiled=True,
    ).astype(jnp.float32)
    query_grad = weight_share[:, :width].astype(jnp.bfloat16)
    key_grad = weight_share[:, width : 2 * width].astype(jnp.bfloat16)
    value_grad = weight_share[:, 2 * width : 3 * width].astype(jnp.bfloat16)
    output_grad = weight_share[:, 3 * width :].T.astype(jnp.bfloat16)
    return (layer_out, input_grad, enc_grad, query_grad, key_grad, value_grad, output_grad)


NZ = 4


def place():
    y, m = lax.axis_index("dp"), lax.axis_index("mp")
    z, x, c = m // 4, (m // 2) % 2, m % 2
    peers = {
        "up": (y, m + 4),
        "down": (y, m - 4),
        "y": (1 - y, m),
        "x": (y, m + 2 - 4 * x),
        "c": (y, m + 1 - 2 * c),
    }
    return y, z, x, c, peers


def when(pred, act):
    if pred is None:
        act()
    else:
        pl.when(pred)(act)


def both(a, b):
    return b if a is None else a if b is None else jnp.logical_and(a, b)


class Sends:
    def __init__(self):
        self.open = []

    def start(self, pred, src, dst, sems, at, peer):
        copy = pltpu.make_async_remote_copy(
            src_ref=src,
            dst_ref=dst,
            send_sem=sems.at[0, at],
            recv_sem=sems.at[1, at],
            device_id=peer,
            device_id_type=MESH,
        )
        when(pred, lambda: copy.start())
        self.open.append((pred, copy))

    def finish(self):
        for pred, copy in self.open:
            when(pred, lambda copy=copy: copy.wait_send())


def arrived(pred, dst, sems, at, peer):
    copy = pltpu.make_async_remote_copy(
        src_ref=dst,
        dst_ref=dst,
        send_sem=sems.at[0, at],
        recv_sem=sems.at[1, at],
        device_id=peer,
        device_id_type=MESH,
    )
    when(pred, lambda: copy.wait_recv())


def feature_block(ref, s, j, x, c):
    return ref.at[s, :, pl.ds(pl.multiple_of(j * 1024 + x * 512 + c * 256, 256), 256)]


def row_block(ref, s, j, x, c):
    return ref.at[s, pl.ds(pl.multiple_of(j * 64 + x * 32 + c * 16, 16), 16), :]


def line_peer(y, z, x, c, d):
    return (y, ((z + d) % NZ) * 4 + x * 2 + c)


def greet(here, peers):
    barrier = pltpu.get_barrier_semaphore()
    targets = [peers[way] for way in ("y", "x", "c")]
    targets += [line_peer(*here, d) for d in range(1, NZ)]
    for target in targets:
        pl.semaphore_signal(barrier, inc=1, device_id=target, device_id_type=MESH)
    pl.semaphore_wait(barrier, len(targets))


def matmul(a, b, dims=((1,), (0,))):
    return lax.dot_general(a, b, (dims, ((), ())), preferred_element_type=F32)


BY_ROWS = ((1,), (1,))
BY_TOKENS = ((0,), (0,))


def chunk(i, size):
    return pl.ds(pl.multiple_of(i * size, size), size)


def diagonal():
    return lax.broadcasted_iota(jnp.int32, (256, 256), 0) == lax.broadcasted_iota(
        jnp.int32, (256, 256), 1
    )


def to_row(column):
    return jnp.sum(jnp.where(diagonal(), column, 0.0), axis=0, keepdims=True)


def to_column(row):
    return jnp.sum(jnp.where(diagonal(), row, 0.0), axis=1, keepdims=True)


def two_rows(first, second):
    upper = lax.broadcasted_iota(jnp.int32, (8, 256), 0) < 4
    return jnp.where(upper, first, second)


GATHER_SEMS, REDUCE_REFS = 5, 12


def kernel(
    enc_len, dec_len, dec, enc, cot, wq_hbm, wk_hbm, wv_hbm, wo_hbm,
    layer_out, input_grad, enc_grad, query_grad, key_grad, value_grad, output_grad,
    masked_own, gd, ge, gc, wq, wk, wv, wo, normed, column, inverse,
    parts, parts_got, grads, po, ng, eg, squares, squares_got, stat,
    stat_got, stat_sum, stat_sems, swap_sems, local_sems, *scratch,
):
    y, z, x, c, peers = place()
    here = (y, z, x, c)
    sends = Sends()

    loads = []
    for i, (src, dst) in enumerate(((wk_hbm, wk), (wv_hbm, wv), (wq_hbm, wq), (wo_hbm, wo))):
        copy = pltpu.make_async_copy(src, dst, local_sems.at[i])
        copy.start()
        loads.append(copy)
    token = lax.broadcasted_iota(jnp.int32, (256, 256), 0)
    masked_own[...] = jnp.where(token < dec_len[0], cot[...].astype(F32), 0.0).astype(BF16)

    gathers = []
    for t, (own, out, rows) in enumerate(((enc, ge, True), (dec, gd, False), (masked_own, gc, False))):
        gathers.append((t, own, out, rows) + tuple(scratch[GATHER_SEMS * t : GATHER_SEMS * (t + 1)]))
    scratch = scratch[3 * GATHER_SEMS :]
    local = [[], [], []]

    def held(tensor, zz):
        _, own, out, rows = tensor[:4]
        if rows:
            return [row_block(out, y, zz, x, c), row_block(out, 2, zz, x, c)]
        slot = y + (2 - y) * ((zz // 2 + y) % 2)
        return [feature_block(out, slot, zz % 2, x, c)]

    def onward(tensor, zz, pred, own=None):
        t, _, out, rows, up, down, ys, xs, cs = tensor
        if rows:
            mine = row_block(out, y, zz, x, c)
            far = row_block(out, 2, zz, x, c)
            src, src_far = (mine, far) if own is None else own
            sends.start(pred, src_far, mine, ys, zz, peers["y"])
            sends.start(pred, src, mine, xs, y * 4 + zz, peers["x"])
            sends.start(pred, src, mine, cs, (y * 4 + zz) * 2 + x, peers["c"])
            return
        other = (zz // 2 + y) % 2
        j = zz % 2
        slot = y + (2 - y) * other
        src = feature_block(out, slot, j, x, c) if own is None else own[0]
        mine = feature_block(out, y, j, x, c)
        sends.start(both(pred, other == 1), src, mine, ys, j, peers["y"])
        near = both(pred, other == 0)
        sends.start(near, src, mine, xs, y * 2 + j, peers["x"])
        sends.start(near, src, mine, cs, (y * 2 + j) * 2 + x, peers["c"])

    def gather_start(tensor):
        t, own, out, rows, up, down = tensor[:6]
        views = held(tensor, z)
        srcs = [own]
        if rows:
            srcs = [own.at[:, chunk(y, 2048)], own.at[:, chunk(1 - y, 2048)]]
        for i, (src, view) in enumerate(zip(srcs, views)):
            sends.start(z < NZ - 1, src, view, up, i, peers["up"])
            sends.start(z > 0, src, view, down, i, peers["down"])
        onward(tensor, z, None, srcs)
        for i, (src, view) in enumerate(zip(srcs, views)):
            copy = pltpu.make_async_copy(src, view, local_sems.at[4 + 2 * t + i])
            copy.start()
            local[t].append(copy)

    def gather_z(tensor):
        t, own, out, rows, up, down = tensor[:6]
        for k in range(NZ - 1):
            below, above = z - 1 - k, z + 1 + k
            for zz, ok, sems_way, way, more in (
                (jnp.maximum(below, 0), below >= 0, up, "up", z < NZ - 1),
                (jnp.minimum(above, NZ - 1), above < NZ, down, "down", z > 0),
            ):
                views = held(tensor, zz)
                n = len(views)
                for i, view in enumerate(views):
                    arrived(ok, view, sems_way, k * n + i, peers["c"])
                    if k + 1 < NZ - 1:
                        sends.start(both(ok, more), view, view, sems_way, (k + 1) * n + i, peers[way])
                onward(tensor, zz, ok)

    def gather_y(tensor):
        t, own, out, rows, up, down, ys, xs, cs = tensor
        block, n = (row_block, 4) if rows else (feature_block, 2)
        for j in range(n):
            view = block(out, 1 - y, j, x, c)
            arrived(None, view, ys, j, peers["y"])
            sends.start(None, view, view, xs, (1 - y) * n + j, peers["x"])
            sends.start(None, view, view, cs, ((1 - y) * n + j) * 2 + x, peers["c"])

    def gather_x(tensor):
        t, own, out, rows, up, down, ys, xs, cs = tensor
        block, n = (row_block, 4) if rows else (feature_block, 2)
        for s in (y, 1 - y):
            for j in range(n):
                view = block(out, s, j, 1 - x, c)
                arrived(None, view, xs, s * n + j, peers["x"])
                sends.start(None, view, view, cs, (s * n + j) * 2 + 1 - x, peers["c"])

    def gather_c(tensor):
        t, own, out, rows, up, down, ys, xs, cs = tensor
        block, n = (row_block, 4) if rows else (feature_block, 2)
        for s in range(2):
            for j in range(n):
                for xx in range(2):
                    arrived(None, block(out, s, j, xx, 1 - c), cs, (s * n + j) * 2 + xx, peers["c"])
        for copy in local[t]:
            copy.wait()

    def project(i, left, weight, dims=((1,), (0,))):
        for s in (1 - y, y):
            parts[i, s] = matmul(left[s], weight[...], dims)
            if s is not y:
                sends.start(None, parts.at[i, s], parts_got.at[i], swap_sems, i, peers["y"])

    def projected(i):
        arrived(None, parts_got.at[i], swap_sems, i, peers["y"])
        return (parts[i, y] + parts_got[i]).astype(BF16)

    greet(here, peers)
    e, d, g = gathers
    gather_start(e)
    gather_start(d)
    gather_z(e)
    gather_start(g)
    gather_y(e)
    gather_z(d)
    gather_x(e)
    gather_y(d)
    gather_z(g)
    gather_c(e)
    loads[0].wait()
    project(0, ge, wk)
    gather_x(d)
    gather_y(g)
    gather_c(d)

    @pl.loop(0, 16)
    def _(i):
        s, rows = i // 8, chunk(i % 8, 32)
        value = gd[s, rows, :].astype(F32)
        total = jnp.sum(value * value, axis=-1, keepdims=True)
        column[s, rows, :] = jnp.broadcast_to(total, (32, 128))

    squares[...] = two_rows(to_row(column[0, :, 0:1]), to_row(column[1, :, 0:1]))
    sends.start(None, squares, squares_got, swap_sems, 8, peers["y"])
    loads[1].wait()
    project(1, ge, wv)
    arrived(None, squares_got, swap_sems, 8, peers["y"])
    features = 16 * dec.shape[1]
    inv_rows = lax.rsqrt((squares[...] + squares_got[...]) / features + 1e-06)
    for s in range(2):
        inverse[s] = jnp.broadcast_to(to_column(inv_rows[4 * s : 4 * s + 1]), (256, 128))

    @pl.loop(0, 16)
    def _(i):
        s, rows = i // 8, chunk(i % 8, 32)
        value = gd[s, rows, :].astype(F32) * inverse[s, rows, 0:1]
        normed[s, rows, :] = value.astype(BF16)

    loads[2].wait()
    project(2, normed, wq)
    gather_x(g)
    gather_c(g)
    loads[3].wait()
    project(3, gc, wo, BY_ROWS)

    scale = DH ** (-0.5)
    keyed = projected(0)
    query = projected(2)
    scores = matmul(query, keyed, BY_ROWS) * scale
    position = lax.broadcasted_iota(jnp.int32, (256, 256), 1)
    scores = jnp.where(position < enc_len[0], scores, -1e30)
    shifted = jnp.exp(scores - jnp.max(scores, axis=-1, keepdims=True))
    probs = shifted / jnp.sum(shifted, axis=-1, keepdims=True)
    probs_low = probs.astype(BF16)
    valued = projected(1)

    def share(i, value):
        grads[i, y] = value.astype(BF16)
        sends.start(None, grads.at[i, y], grads.at[i, y], swap_sems, 4 + i, peers["y"])

    def shared(i):
        arrived(None, grads.at[i, 1 - y], swap_sems, 4 + i, peers["y"])

    ATT, QG, KG, VG = range(4)
    share(ATT, matmul(probs_low, valued))
    attended_grad = projected(3)
    probs_grad = matmul(attended_grad, valued, BY_ROWS)
    scores_grad = (
        probs * (probs_grad - jnp.sum(probs * probs_grad, axis=-1, keepdims=True)) * scale
    ).astype(BF16)
    share(QG, matmul(scores_grad, keyed))
    share(KG, matmul(scores_grad, query, BY_TOKENS))
    share(VG, matmul(probs_low, attended_grad, BY_TOKENS))

    reduces = []
    for t, (part, rows) in enumerate(((po, False), (ng, False), (eg, True))):
        reduces.append((part, rows) + tuple(scratch[REDUCE_REFS * t : REDUCE_REFS * (t + 1)]))

    def across_core(tensor, s):
        part, rows, rc, ax, rx, by, ry, v, sz, rz, cs, xs, ys, zs = tensor
        block, n = (row_block, 4) if rows else (feature_block, 2)
        for xx in (1 - x, x):
            for j in range(n):
                at = (s * n + j) * 2 + xx
                sends.start(None, block(part, s, j, xx, 1 - c), rc.at[at], cs, at, peers["c"])

    def across_x(tensor, s):
        part, rows, rc, ax, rx, by, ry, v, sz, rz, cs, xs, ys, zs = tensor
        block, n = (row_block, 4) if rows else (feature_block, 2)
        for j in range(n):
            at = (s * n + j) * 2 + 1 - x
            arrived(None, rc.at[at], cs, at, peers["c"])
            own = block(part, s, j, 1 - x, c)[...].astype(F32)
            ax[s * n + j] = (own + rc[at].astype(F32)).astype(BF16)
            sends.start(None, ax.at[s * n + j], rx.at[s * n + j], xs, s * n + j, peers["x"])

    def across_y(tensor, theirs):
        part, rows, rc, ax, rx, by, ry, v, sz, rz, cs, xs, ys, zs = tensor
        block, n = (row_block, 4) if rows else (feature_block, 2)
        s = 1 - y if theirs else y
        for j in range(n):
            at = (s * n + j) * 2 + x
            arrived(None, rc.at[at], cs, at, peers["c"])
            arrived(None, rx.at[s * n + j], xs, s * n + j, peers["x"])
            own = block(part, s, j, x, c)[...].astype(F32)
            total = own + rc[at].astype(F32) + rx[s * n + j].astype(F32)
            if theirs:
                by[j] = total.astype(BF16)
                sends.start(None, by.at[j], ry.at[j], ys, j, peers["y"])
            elif rows:
                v[j, :, chunk(y, 2048)] = total
            else:
                v[2 * y + j] = total

    def along_z(tensor):
        part, rows, rc, ax, rx, by, ry, v, sz, rz, cs, xs, ys, zs = tensor
        n = 4 if rows else 2
        for j in range(n):
            arrived(None, ry.at[j], ys, j, peers["y"])
            if rows:
                v[j, :, chunk(1 - y, 2048)] = ry[j].astype(F32)
            else:
                v[2 * (1 - y) + j] = ry[j].astype(F32)
        for step in (2, 1, 3):
            sz[step - 1] = v[(z + step) % NZ].astype(BF16)
            sends.start(
                None, sz.at[step - 1], rz.at[step - 1], zs, step - 1, line_peer(*here, step)
            )

    def summed(tensor):
        part, rows, rc, ax, rx, by, ry, v, sz, rz, cs, xs, ys, zs = tensor
        total = v[z]
        for step in range(1, NZ):
            arrived(None, rz.at[step - 1], zs, step - 1, peers["c"])
            total += rz[step - 1].astype(F32)
        return total

    def stat_step(k, way):
        arrived(None, stat_got.at[k], stat_sems, k, peers["c"])
        before = stat[...] if k == 0 else stat_sum[k - 1]
        stat_sum[k] = before + stat_got[k]
        if way:
            sends.start(None, stat_sum.at[k], stat_got.at[k + 1], stat_sems, k + 1, peers[way])

    def out_parts(s):
        @pl.loop(0, 4)
        def _(i):
            po[s, :, chunk(i, 512)] = matmul(grads[ATT, s], wo[:, chunk(i, 512)]).astype(BF16)

    def normed_parts(s):
        column[s] = jnp.zeros((256, 128), F32)

        @pl.loop(0, 8)
        def _(i):
            cols = chunk(i, 256)
            part = matmul(grads[QG, s], wq[cols, :], BY_ROWS).astype(BF16)
            ng[s, :, cols] = part
            dots = jnp.sum(part.astype(F32) * gd[s, :, cols].astype(F32), axis=-1, keepdims=True)
            column[s] += jnp.broadcast_to(dots, (256, 128))

    def enc_parts(s):
        @pl.loop(0, 4)
        def _(i):
            cols = chunk(i, 512)
            total = matmul(grads[KG, s], wk[cols, :], BY_ROWS)
            total += matmul(grads[VG, s], wv[cols, :], BY_ROWS)
            eg[s, :, cols] = total.astype(BF16)

    def weight_part(out, left, i):
        @pl.loop(0, 8)
        def _(step):
            rows = chunk(step, 256)
            total = matmul(left[0, :, rows], grads[i, 0], BY_TOKENS)
            total += matmul(left[1, :, rows], grads[i, 1], BY_TOKENS)
            out[rows, :] = total.astype(BF16)

    ro, rn, re = reduces
    out_parts(y)
    across_core(ro, y)
    normed_parts(y)
    across_core(rn, y)
    across_x(ro, y)
    shared(ATT)
    out_parts(1 - y)
    across_core(ro, 1 - y)
    shared(QG)
    across_x(rn, y)
    normed_parts(1 - y)
    across_core(rn, 1 - y)
    across_x(ro, 1 - y)
    stat[...] = two_rows(to_row(column[0, :, 0:1]), to_row(column[1, :, 0:1]))
    sends.start(None, stat, stat_got.at[0], stat_sems, 0, peers["c"])
    shared(KG)
    shared(VG)
    enc_parts(1 - y)
    across_core(re, 1 - y)
    across_x(rn, 1 - y)
    enc_parts(y)
    across_core(re, y)
    stat_step(0, "x")
    across_x(re, 1 - y)
    across_x(re, y)
    weight_part(query_grad, normed, QG)
    across_y(ro, True)
    across_y(ro, False)
    stat_step(1, "y")
    weight_part(key_grad, ge, KG)
    along_z(ro)
    across_y(rn, True)
    across_y(rn, False)
    stat_step(2, None)
    for step in range(1, NZ):
        sends.start(
            None, stat_sum.at[2], stat_got.at[2 + step], stat_sems, 2 + step, line_peer(*here, step)
        )
    along_z(rn)
    weight_part(value_grad, ge, VG)
    across_y(re, True)
    across_y(re, False)
    along_z(re)

    @pl.loop(0, 4)
    def _(i):
        cols = chunk(i, 512)
        total = matmul(grads[ATT, 0], gc[0, :, cols], BY_TOKENS)
        total += matmul(grads[ATT, 1], gc[1, :, cols], BY_TOKENS)
        output_grad[:, cols] = total.astype(BF16)

    layer_out[...] = (dec[...].astype(F32) + summed(ro)).astype(BF16)
    total = stat_sum[2]
    for step in range(1, NZ):
        arrived(None, stat_got.at[2 + step], stat_sems, 2 + step, peers["c"])
        total += stat_got[2 + step]
    mean = to_column(jnp.where(y == 0, total[0:1], total[4:5])) / features
    inv = inverse[y][:, 0:1]
    input_grad[...] = (
        masked_own[...].astype(F32)
        + inv * summed(rn)
        - dec[...].astype(F32) * (inv * inv * inv) * mean
    ).astype(BF16)
    enc_grad[...] = summed(re).astype(BF16)
    sends.finish()


def fast(
    dec_input,
    enc_output,
    query_weight,
    key_weight,
    value_weight,
    output_weight,
    cotangent,
    enc_lengths,
    dec_lengths,
):
    vmem = pl.BlockSpec(memory_space=pltpu.VMEM)
    smem = pl.BlockSpec(memory_space=pltpu.SMEM)
    hbm = pl.BlockSpec(memory_space=pl.ANY)
    dma = lambda *shape: pltpu.SemaphoreType.DMA(shape)
    scratch = [
        pltpu.VMEM((256, 256), BF16),
        pltpu.VMEM((3, 256, 2048), BF16),
        pltpu.VMEM((3, 256, 2048), BF16),
        pltpu.VMEM((3, 256, 2048), BF16),
        pltpu.VMEM((2048, 256), BF16),
        pltpu.VMEM((2048, 256), BF16),
        pltpu.VMEM((2048, 256), BF16),
        pltpu.VMEM((256, 2048), BF16),
        pltpu.VMEM((2, 256, 2048), BF16),
        pltpu.VMEM((2, 256, 128), F32),
        pltpu.VMEM((2, 256, 128), F32),
        pltpu.VMEM((4, 2, 256, 256), F32),
        pltpu.VMEM((4, 256, 256), F32),
        pltpu.VMEM((4, 2, 256, 256), BF16),
        pltpu.VMEM((2, 256, 2048), BF16),
        pltpu.VMEM((2, 256, 2048), BF16),
        pltpu.VMEM((2, 256, 2048), BF16),
        pltpu.VMEM((8, 256), F32),
        pltpu.VMEM((8, 256), F32),
        pltpu.VMEM((8, 256), F32),
        pltpu.VMEM((6, 8, 256), F32),
        pltpu.VMEM((3, 8, 256), F32),
        dma(2, 6),
        dma(2, 9),
        dma(10),
    ]
    for n in (2, 1, 1):
        scratch += [dma(2, count * n) for count in (3, 3, 2, 4, 8)]
    for rows in (False, False, True):
        n = 4 if rows else 2
        r, w, wz = (16, 2048, 4096) if rows else (256, 256, 256)
        scratch += [
            pltpu.VMEM((4 * n, r, w), BF16),
            pltpu.VMEM((2 * n, r, w), BF16),
            pltpu.VMEM((2 * n, r, w), BF16),
            pltpu.VMEM((n, r, w), BF16),
            pltpu.VMEM((n, r, w), BF16),
            pltpu.VMEM((NZ, r, wz), F32),
        ]
        scratch += [pltpu.VMEM((NZ - 1, r, wz), BF16)] * 2
        scratch += [dma(2, k) for k in (4 * n, 2 * n, n, NZ - 1)]
    shapes = ((256, 256), (256, 256), (16, 4096)) + ((2048, 256),) * 3 + ((256, 2048),)
    results = pl.pallas_call(
        kernel,
        out_shape=tuple(jax.ShapeDtypeStruct(shape, BF16) for shape in shapes),
        in_specs=[smem, smem, vmem, vmem, vmem, hbm, hbm, hbm, hbm],
        out_specs=(vmem,) * 7,
        scratch_shapes=scratch,
        compiler_params=pltpu.CompilerParams(
            collective_id=0, has_side_effects=True, vmem_limit_bytes=58 * 2**20
        ),
        name="cross_attention",
    )(
        enc_lengths, dec_lengths, dec_input[0], enc_output[0], cotangent[0],
        query_weight, key_weight, value_weight, output_weight,
    )
    return tuple(out[None] for out in results[:3]) + tuple(results[3:])


def solution(mesh):
    in_specs = (
        P("dp", None, "mp"),
        P("dp", "mp", None),
        P("dp", "mp"),
        P("dp", "mp"),
        P("dp", "mp"),
        P("mp", "dp"),
        P("dp", None, "mp"),
        P("dp"),
        P("dp"),
    )
    out_specs = (
        P("dp", None, "mp"),
        P("dp", None, "mp"),
        P("dp", "mp", None),
        P("dp", "mp"),
        P("dp", "mp"),
        P("dp", "mp"),
        P("mp", "dp"),
    )
    program = fast if dict(mesh.shape) == {"dp": 2, "mp": 16} else local
    return jax.shard_map(program, mesh=mesh, in_specs=in_specs, out_specs=out_specs, check_vma=False)
```

```python
import functools

import jax
import jax.numpy as jnp
from jax import lax
from jax.experimental import pallas as pl
from jax.experimental.pallas import tpu as pltpu
from jax.sharding import PartitionSpec as P

DH = 256
MESH = pl.DeviceIdType.MESH
F32 = jnp.float32
BF16 = jnp.bfloat16


def local(
    dec_input,
    enc_output,
    query_weight,
    key_weight,
    value_weight,
    output_weight,
    cotangent,
    enc_lengths,
    dec_lengths,
):
    scale = DH ** (-0.5)
    hidden = lax.all_gather(dec_input, "mp", axis=2, tiled=True)[0]
    query_full, key_full, value_full = (
        lax.all_gather(query_weight, "dp", axis=0, tiled=True),
        lax.all_gather(key_weight, "dp", axis=0, tiled=True),
        lax.all_gather(value_weight, "dp", axis=0, tiled=True),
    )
    output_full = lax.all_gather(output_weight, "dp", axis=1, tiled=True)
    encoded = lax.all_gather(enc_output, "mp", axis=1, tiled=True)[0]
    tokens = hidden.shape[0]
    keys_len = encoded.shape[0]
    width = query_weight.shape[1]
    heads_here = width // DH
    hidden32 = hidden.astype(jnp.float32)
    inv_rms = lax.rsqrt(jnp.mean(hidden32 * hidden32, axis=-1, keepdims=True) + 1e-06)
    normed = (hidden32 * inv_rms).astype(jnp.bfloat16)
    query = jnp.dot(normed, query_full, preferred_element_type=jnp.float32).astype(jnp.bfloat16)
    keyed = jnp.dot(encoded, key_full, preferred_element_type=jnp.float32).astype(jnp.bfloat16)
    valued = jnp.dot(encoded, value_full, preferred_element_type=jnp.float32).astype(jnp.bfloat16)
    query_heads = query.reshape(tokens, heads_here, DH)
    key_heads = keyed.reshape(keys_len, heads_here, DH)
    value_heads = valued.reshape(keys_len, heads_here, DH)
    scores = (
        jnp.einsum("thd,lhd->htl", query_heads, key_heads, preferred_element_type=jnp.float32)
        * scale
    )
    valid = jnp.arange(keys_len, dtype=jnp.int32) < enc_lengths[0]
    scores = jnp.where(valid[None, None, :], scores, -1e30)
    shifted = jnp.exp(scores - jnp.max(scores, axis=-1, keepdims=True))
    probs = shifted / jnp.sum(shifted, axis=-1, keepdims=True)
    probs_low = probs.astype(jnp.bfloat16)
    attended = (
        jnp.einsum("htl,lhd->thd", probs_low, value_heads, preferred_element_type=jnp.float32)
        .reshape(tokens, width)
        .astype(jnp.bfloat16)
    )
    partial_out = jnp.dot(attended, output_full, preferred_element_type=jnp.float32)
    out_share = lax.psum_scatter(
        partial_out.astype(jnp.bfloat16), "mp", scatter_dimension=1, tiled=True
    ).astype(jnp.float32)
    own_input = dec_input[0].astype(jnp.float32)
    layer_out = (own_input + out_share).astype(jnp.bfloat16)[None]
    upstream = lax.all_gather(cotangent, "mp", axis=2, tiled=True)[0]
    keep = (jnp.arange(tokens, dtype=jnp.int32) < dec_lengths[0])[:, None]
    masked = jnp.where(keep, upstream, jnp.zeros_like(upstream))
    own_masked = jnp.where(keep, cotangent[0], jnp.zeros_like(cotangent[0]))
    attended_grad = jnp.dot(masked, output_full.T, preferred_element_type=jnp.float32).astype(
        jnp.bfloat16
    )
    grad_heads = attended_grad.reshape(tokens, heads_here, DH)
    probs_grad = jnp.einsum(
        "thd,lhd->htl", grad_heads, value_heads, preferred_element_type=jnp.float32
    )
    scores_grad = (
        probs * (probs_grad - jnp.sum(probs * probs_grad, axis=-1, keepdims=True)) * scale
    ).astype(jnp.bfloat16)
    q_grad = (
        jnp.einsum("htl,lhd->thd", scores_grad, key_heads, preferred_element_type=jnp.float32)
        .reshape(tokens, width)
        .astype(jnp.bfloat16)
    )
    k_grad = (
        jnp.einsum("htl,thd->lhd", scores_grad, query_heads, preferred_element_type=jnp.float32)
        .reshape(keys_len, width)
        .astype(jnp.bfloat16)
    )
    v_grad = (
        jnp.einsum("htl,thd->lhd", probs_low, grad_heads, preferred_element_type=jnp.float32)
        .reshape(keys_len, width)
        .astype(jnp.bfloat16)
    )
    normed_part = jnp.dot(q_grad, query_full.T, preferred_element_type=jnp.float32)
    feature_width = dec_input.shape[2]
    normed_grad = lax.psum(normed_part.astype(jnp.bfloat16), "mp").astype(jnp.float32)
    stat = jnp.mean(normed_grad * hidden32, axis=-1, keepdims=True)
    full_grad = inv_rms * normed_grad - hidden32 * inv_rms**3 * stat
    start = lax.axis_index("mp") * feature_width
    input_share = lax.dynamic_slice_in_dim(full_grad, start, feature_width, 1)
    input_grad = (own_masked.astype(jnp.float32) + input_share).astype(jnp.bfloat16)[None]
    enc_share = lax.psum_scatter(
        (
            jnp.dot(k_grad, key_full.T, preferred_element_type=jnp.float32)
            + jnp.dot(v_grad, value_full.T, preferred_element_type=jnp.float32)
        ).astype(jnp.bfloat16),
        "mp",
        scatter_dimension=0,
        tiled=True,
    )
    enc_grad = enc_share[None]
    weight_share = lax.psum_scatter(
        jnp.concatenate(
            [
                jnp.dot(normed.T, q_grad, preferred_element_type=jnp.float32),
                jnp.dot(encoded.T, k_grad, preferred_element_type=jnp.float32),
                jnp.dot(encoded.T, v_grad, preferred_element_type=jnp.float32),
                jnp.dot(masked.T, attended, preferred_element_type=jnp.float32),
            ],
            axis=1,
        ).astype(jnp.bfloat16),
        "dp",
        scatter_dimension=0,
        tiled=True,
    ).astype(jnp.float32)
    query_grad = weight_share[:, :width].astype(jnp.bfloat16)
    key_grad = weight_share[:, width : 2 * width].astype(jnp.bfloat16)
    value_grad = weight_share[:, 2 * width : 3 * width].astype(jnp.bfloat16)
    output_grad = weight_share[:, 3 * width :].T.astype(jnp.bfloat16)
    return (layer_out, input_grad, enc_grad, query_grad, key_grad, value_grad, output_grad)


NZ = 4


def place():
    y, m = lax.axis_index("dp"), lax.axis_index("mp")
    z, x, c = m // 4, (m // 2) % 2, m % 2
    peers = {
        "up": (y, m + 4),
        "down": (y, m - 4),
        "y": (1 - y, m),
        "x": (y, m + 2 - 4 * x),
        "c": (y, m + 1 - 2 * c),
    }
    return y, z, x, c, peers


def when(pred, act):
    if pred is None:
        act()
    else:
        pl.when(pred)(act)


def both(a, b):
    return b if a is None else a if b is None else jnp.logical_and(a, b)


class Sends:
    def __init__(self):
        self.open = []

    def start(self, pred, src, dst, sems, at, peer):
        copy = pltpu.make_async_remote_copy(
            src_ref=src,
            dst_ref=dst,
            send_sem=sems.at[0, at],
            recv_sem=sems.at[1, at],
            device_id=peer,
            device_id_type=MESH,
        )
        when(pred, lambda: copy.start())
        self.open.append((pred, copy))

    def finish(self):
        for pred, copy in self.open:
            when(pred, lambda copy=copy: copy.wait_send())


def arrived(pred, dst, sems, at, peer):
    copy = pltpu.make_async_remote_copy(
        src_ref=dst,
        dst_ref=dst,
        send_sem=sems.at[0, at],
        recv_sem=sems.at[1, at],
        device_id=peer,
        device_id_type=MESH,
    )
    when(pred, lambda: copy.wait_recv())


def feature_block(ref, s, j, x, c):
    return ref.at[s, :, pl.ds(pl.multiple_of(j * 1024 + x * 512 + c * 256, 256), 256)]


def row_block(ref, s, j, x, c):
    return ref.at[s, pl.ds(pl.multiple_of(j * 64 + x * 32 + c * 16, 16), 16), :]


def line_peer(y, z, x, c, d):
    return (y, ((z + d) % NZ) * 4 + x * 2 + c)


def greet(here, peers):
    barrier = pltpu.get_barrier_semaphore()
    targets = [peers[way] for way in ("y", "x", "c")]
    targets += [line_peer(*here, d) for d in range(1, NZ)]
    for target in targets:
        pl.semaphore_signal(barrier, inc=1, device_id=target, device_id_type=MESH)
    pl.semaphore_wait(barrier, len(targets))


def matmul(a, b, dims=((1,), (0,))):
    return lax.dot_general(a, b, (dims, ((), ())), preferred_element_type=F32)


BY_ROWS = ((1,), (1,))
BY_TOKENS = ((0,), (0,))


def chunk(i, size):
    return pl.ds(pl.multiple_of(i * size, size), size)


def diagonal():
    return lax.broadcasted_iota(jnp.int32, (256, 256), 0) == lax.broadcasted_iota(
        jnp.int32, (256, 256), 1
    )


def to_row(column):
    return jnp.sum(jnp.where(diagonal(), column, 0.0), axis=0, keepdims=True)


def to_column(row):
    return jnp.sum(jnp.where(diagonal(), row, 0.0), axis=1, keepdims=True)


def two_rows(first, second):
    upper = lax.broadcasted_iota(jnp.int32, (8, 256), 0) < 4
    return jnp.where(upper, first, second)


GATHER_SEMS, REDUCE_REFS = 5, 12


def kernel(
    enc_len, dec_len, dec, enc, cot, wq_hbm, wk_hbm, wv_hbm, wo_hbm,
    layer_out, input_grad, enc_grad, query_out, key_out, value_out, output_out,
    query_grad, key_grad, value_grad, output_grad, masked_own, gd, ge, gc, wq, wk, wv, wo, normed, column, inverse,
    parts, parts_got, grads, po, ng, eg, squares, squares_got, stat,
    stat_got, stat_sum, stat_sems, swap_sems, local_sems, *scratch,
):
    y, z, x, c, peers = place()
    here = (y, z, x, c)
    sends = Sends()

    loads = []
    for i, (src, dst) in enumerate(((wk_hbm, wk), (wv_hbm, wv), (wq_hbm, wq), (wo_hbm, wo))):
        copy = pltpu.make_async_copy(src, dst, local_sems.at[i])
        copy.start()
        loads.append(copy)
    token = lax.broadcasted_iota(jnp.int32, (256, 256), 0)
    masked_own[...] = jnp.where(token < dec_len[0], cot[...].astype(F32), 0.0).astype(BF16)

    gathers = []
    for t, (own, out, rows) in enumerate(((enc, ge, True), (dec, gd, False), (masked_own, gc, False))):
        gathers.append((t, own, out, rows) + tuple(scratch[GATHER_SEMS * t : GATHER_SEMS * (t + 1)]))
    scratch = scratch[3 * GATHER_SEMS :]
    local = [[], [], []]

    def held(tensor, zz):
        _, own, out, rows = tensor[:4]
        if rows:
            return [row_block(out, y, zz, x, c), row_block(out, 2, zz, x, c)]
        slot = y + (2 - y) * ((zz // 2 + y) % 2)
        return [feature_block(out, slot, zz % 2, x, c)]

    def onward(tensor, zz, pred, own=None):
        t, _, out, rows, up, down, ys, xs, cs = tensor
        if rows:
            mine = row_block(out, y, zz, x, c)
            far = row_block(out, 2, zz, x, c)
            src, src_far = (mine, far) if own is None else own
            sends.start(pred, src_far, mine, ys, zz, peers["y"])
            sends.start(pred, src, mine, xs, y * 4 + zz, peers["x"])
            sends.start(pred, src, mine, cs, (y * 4 + zz) * 2 + x, peers["c"])
            return
        other = (zz // 2 + y) % 2
        j = zz % 2
        slot = y + (2 - y) * other
        src = feature_block(out, slot, j, x, c) if own is None else own[0]
        mine = feature_block(out, y, j, x, c)
        sends.start(both(pred, other == 1), src, mine, ys, j, peers["y"])
        near = both(pred, other == 0)
        sends.start(near, src, mine, xs, y * 2 + j, peers["x"])
        sends.start(near, src, mine, cs, (y * 2 + j) * 2 + x, peers["c"])

    def gather_start(tensor):
        t, own, out, rows, up, down = tensor[:6]
        views = held(tensor, z)
        srcs = [own]
        if rows:
            srcs = [own.at[:, chunk(y, 2048)], own.at[:, chunk(1 - y, 2048)]]
        for i, (src, view) in enumerate(zip(srcs, views)):
            sends.start(z < NZ - 1, src, view, up, i, peers["up"])
            sends.start(z > 0, src, view, down, i, peers["down"])
        onward(tensor, z, None, srcs)
        for i, (src, view) in enumerate(zip(srcs, views)):
            copy = pltpu.make_async_copy(src, view, local_sems.at[4 + 2 * t + i])
            copy.start()
            local[t].append(copy)

    def gather_z(tensor):
        t, own, out, rows, up, down = tensor[:6]
        for k in range(NZ - 1):
            below, above = z - 1 - k, z + 1 + k
            for zz, ok, sems_way, way, more in (
                (jnp.maximum(below, 0), below >= 0, up, "up", z < NZ - 1),
                (jnp.minimum(above, NZ - 1), above < NZ, down, "down", z > 0),
            ):
                views = held(tensor, zz)
                n = len(views)
                for i, view in enumerate(views):
                    arrived(ok, view, sems_way, k * n + i, peers["c"])
                    if k + 1 < NZ - 1:
                        sends.start(both(ok, more), view, view, sems_way, (k + 1) * n + i, peers[way])
                onward(tensor, zz, ok)

    def gather_y(tensor):
        t, own, out, rows, up, down, ys, xs, cs = tensor
        block, n = (row_block, 4) if rows else (feature_block, 2)
        for j in range(n):
            view = block(out, 1 - y, j, x, c)
            arrived(None, view, ys, j, peers["y"])
            sends.start(None, view, view, xs, (1 - y) * n + j, peers["x"])
            sends.start(None, view, view, cs, ((1 - y) * n + j) * 2 + x, peers["c"])

    def gather_x(tensor):
        t, own, out, rows, up, down, ys, xs, cs = tensor
        block, n = (row_block, 4) if rows else (feature_block, 2)
        for s in (y, 1 - y):
            for j in range(n):
                view = block(out, s, j, 1 - x, c)
                arrived(None, view, xs, s * n + j, peers["x"])
                sends.start(None, view, view, cs, (s * n + j) * 2 + 1 - x, peers["c"])

    def gather_c(tensor):
        t, own, out, rows, up, down, ys, xs, cs = tensor
        block, n = (row_block, 4) if rows else (feature_block, 2)
        for s in range(2):
            for j in range(n):
                for xx in range(2):
                    arrived(None, block(out, s, j, xx, 1 - c), cs, (s * n + j) * 2 + xx, peers["c"])
        for copy in local[t]:
            copy.wait()

    def project(i, left, weight, dims=((1,), (0,))):
        for s in (1 - y, y):
            parts[i, s] = matmul(left[s], weight[...], dims)
            if s is not y:
                sends.start(None, parts.at[i, s], parts_got.at[i], swap_sems, i, peers["y"])

    def projected(i):
        arrived(None, parts_got.at[i], swap_sems, i, peers["y"])
        return (parts[i, y] + parts_got[i]).astype(BF16)

    greet(here, peers)
    e, d, g = gathers
    gather_start(e)
    gather_start(d)
    gather_z(e)
    gather_start(g)
    gather_y(e)
    gather_z(d)
    gather_x(e)
    gather_y(d)
    gather_z(g)
    gather_c(e)
    loads[0].wait()
    project(0, ge, wk)
    gather_x(d)
    gather_y(g)
    gather_c(d)

    @pl.loop(0, 16)
    def _(i):
        s, rows = i // 8, chunk(i % 8, 32)
        value = gd[s, rows, :].astype(F32)
        total = jnp.sum(value * value, axis=-1, keepdims=True)
        column[s, rows, :] = jnp.broadcast_to(total, (32, 128))

    squares[...] = two_rows(to_row(column[0, :, 0:1]), to_row(column[1, :, 0:1]))
    sends.start(None, squares, squares_got, swap_sems, 8, peers["y"])
    loads[1].wait()
    project(1, ge, wv)
    arrived(None, squares_got, swap_sems, 8, peers["y"])
    features = 16 * dec.shape[1]
    inv_rows = lax.rsqrt((squares[...] + squares_got[...]) / features + 1e-06)
    for s in range(2):
        inverse[s] = jnp.broadcast_to(to_column(inv_rows[4 * s : 4 * s + 1]), (256, 128))

    @pl.loop(0, 16)
    def _(i):
        s, rows = i // 8, chunk(i % 8, 32)
        value = gd[s, rows, :].astype(F32) * inverse[s, rows, 0:1]
        normed[s, rows, :] = value.astype(BF16)

    loads[2].wait()
    project(2, normed, wq)
    gather_x(g)

    ATT, QG, KG, VG = range(4)

    def share(i, value):
        grads[i, y] = value.astype(BF16)
        sends.start(None, grads.at[i, y], grads.at[i, y], swap_sems, 4 + i, peers["y"])

    def shared(i):
        arrived(None, grads.at[i, 1 - y], swap_sems, 4 + i, peers["y"])

    scale = DH ** (-0.5)
    keyed = projected(0)
    query = projected(2)
    scores = matmul(query, keyed, BY_ROWS) * scale
    position = lax.broadcasted_iota(jnp.int32, (256, 256), 1)
    scores = jnp.where(position < enc_len[0], scores, -1e30)
    shifted = jnp.exp(scores - jnp.max(scores, axis=-1, keepdims=True))
    probs = shifted / jnp.sum(shifted, axis=-1, keepdims=True)
    probs_low = probs.astype(BF16)
    valued = projected(1)
    share(ATT, matmul(probs_low, valued))
    gather_c(g)
    loads[3].wait()
    project(3, gc, wo, BY_ROWS)

    reduces = []
    for t, (part, rows) in enumerate(((po, False), (ng, False), (eg, True))):
        reduces.append((part, rows) + tuple(scratch[REDUCE_REFS * t : REDUCE_REFS * (t + 1)]))

    def across_core(tensor, s):
        part, rows, rc, ax, rx, by, ry, v, sz, rz, cs, xs, ys, zs = tensor
        block, n = (row_block, 4) if rows else (feature_block, 2)
        for xx in (1 - x, x):
            for j in range(n):
                at = (s * n + j) * 2 + xx
                sends.start(None, block(part, s, j, xx, 1 - c), rc.at[at], cs, at, peers["c"])

    def across_x(tensor, s):
        part, rows, rc, ax, rx, by, ry, v, sz, rz, cs, xs, ys, zs = tensor
        block, n = (row_block, 4) if rows else (feature_block, 2)
        for j in range(n):
            at = (s * n + j) * 2 + 1 - x
            arrived(None, rc.at[at], cs, at, peers["c"])
            own = block(part, s, j, 1 - x, c)[...].astype(F32)
            ax[s * n + j] = (own + rc[at].astype(F32)).astype(BF16)
            sends.start(None, ax.at[s * n + j], rx.at[s * n + j], xs, s * n + j, peers["x"])

    def across_y(tensor, theirs):
        part, rows, rc, ax, rx, by, ry, v, sz, rz, cs, xs, ys, zs = tensor
        block, n = (row_block, 4) if rows else (feature_block, 2)
        s = 1 - y if theirs else y
        for j in range(n):
            at = (s * n + j) * 2 + x
            arrived(None, rc.at[at], cs, at, peers["c"])
            arrived(None, rx.at[s * n + j], xs, s * n + j, peers["x"])
            own = block(part, s, j, x, c)[...].astype(F32)
            total = own + rc[at].astype(F32) + rx[s * n + j].astype(F32)
            if theirs:
                by[j] = total.astype(BF16)
                sends.start(None, by.at[j], ry.at[j], ys, j, peers["y"])
            elif rows:
                v[j, :, chunk(y, 2048)] = total
            else:
                v[2 * y + j] = total

    def along_z(tensor):
        part, rows, rc, ax, rx, by, ry, v, sz, rz, cs, xs, ys, zs = tensor
        n = 4 if rows else 2
        for j in range(n):
            arrived(None, ry.at[j], ys, j, peers["y"])
            if rows:
                v[j, :, chunk(1 - y, 2048)] = ry[j].astype(F32)
            else:
                v[2 * (1 - y) + j] = ry[j].astype(F32)
        for step in (2, 1, 3):
            sz[step - 1] = v[(z + step) % NZ].astype(BF16)
            sends.start(
                None, sz.at[step - 1], rz.at[step - 1], zs, step - 1, line_peer(*here, step)
            )

    def summed(tensor):
        part, rows, rc, ax, rx, by, ry, v, sz, rz, cs, xs, ys, zs = tensor
        total = v[z]
        for step in range(1, NZ):
            arrived(None, rz.at[step - 1], zs, step - 1, peers["c"])
            total += rz[step - 1].astype(F32)
        return total

    def stat_step(k, way):
        arrived(None, stat_got.at[k], stat_sems, k, peers["c"])
        before = stat[...] if k == 0 else stat_sum[k - 1]
        stat_sum[k] = before + stat_got[k]
        if way:
            sends.start(None, stat_sum.at[k], stat_got.at[k + 1], stat_sems, k + 1, peers[way])

    def emit(i, value):
        out = (output_out, query_out, key_out, value_out)[i]
        copy = pltpu.make_async_copy(value, out, local_sems.at[10 + i])
        copy.start()
        loads.append(copy)

    def out_parts(s):
        @pl.loop(0, 4)
        def _(i):
            po[s, :, chunk(i, 512)] = matmul(grads[ATT, s], wo[:, chunk(i, 512)]).astype(BF16)

    def normed_parts(s):
        column[s] = jnp.zeros((256, 128), F32)

        @pl.loop(0, 8)
        def _(i):
            cols = chunk(i, 256)
            part = matmul(grads[QG, s], wq[cols, :], BY_ROWS).astype(BF16)
            ng[s, :, cols] = part
            dots = jnp.sum(part.astype(F32) * gd[s, :, cols].astype(F32), axis=-1, keepdims=True)
            column[s] += jnp.broadcast_to(dots, (256, 128))

    def enc_parts(s):
        @pl.loop(0, 4)
        def _(i):
            cols = chunk(i, 512)
            total = matmul(grads[KG, s], wk[cols, :], BY_ROWS)
            total += matmul(grads[VG, s], wv[cols, :], BY_ROWS)
            eg[s, :, cols] = total.astype(BF16)

    def weight_part(out, left, i):
        @pl.loop(0, 8)
        def _(step):
            rows = chunk(step, 256)
            total = matmul(left[0, :, rows], grads[i, 0], BY_TOKENS)
            total += matmul(left[1, :, rows], grads[i, 1], BY_TOKENS)
            out[rows, :] = total.astype(BF16)

        emit(i, out)

    ro, rn, re = reduces
    out_parts(y)
    across_core(ro, y)
    shared(ATT)
    out_parts(1 - y)
    across_core(ro, 1 - y)
    across_x(ro, y)
    across_x(ro, 1 - y)

    attended_grad = projected(3)
    probs_grad = matmul(attended_grad, valued, BY_ROWS)
    scores_grad = (
        probs * (probs_grad - jnp.sum(probs * probs_grad, axis=-1, keepdims=True)) * scale
    ).astype(BF16)
    share(QG, matmul(scores_grad, keyed))
    share(KG, matmul(scores_grad, query, BY_TOKENS))
    share(VG, matmul(probs_low, attended_grad, BY_TOKENS))
    normed_parts(y)
    across_core(rn, y)
    enc_parts(y)
    across_core(re, y)
    across_x(rn, y)
    shared(QG)
    normed_parts(1 - y)
    across_core(rn, 1 - y)
    stat[...] = two_rows(to_row(column[0, :, 0:1]), to_row(column[1, :, 0:1]))
    sends.start(None, stat, stat_got.at[0], stat_sems, 0, peers["c"])
    across_x(re, y)
    shared(KG)
    shared(VG)
    enc_parts(1 - y)
    across_core(re, 1 - y)
    across_x(rn, 1 - y)
    across_y(ro, True)
    across_y(ro, False)
    stat_step(0, "x")
    across_x(re, 1 - y)
    along_z(ro)
    weight_part(query_grad, normed, QG)
    stat_step(1, "y")
    weight_part(key_grad, ge, KG)
    across_y(rn, True)
    across_y(rn, False)
    stat_step(2, None)
    for step in range(1, NZ):
        sends.start(
            None, stat_sum.at[2], stat_got.at[2 + step], stat_sems, 2 + step, line_peer(*here, step)
        )
    along_z(rn)
    weight_part(value_grad, ge, VG)
    across_y(re, True)
    across_y(re, False)
    along_z(re)

    @pl.loop(0, 4)
    def _(i):
        cols = chunk(i, 512)
        total = matmul(grads[ATT, 0], gc[0, :, cols], BY_TOKENS)
        total += matmul(grads[ATT, 1], gc[1, :, cols], BY_TOKENS)
        output_grad[:, cols] = total.astype(BF16)

    emit(ATT, output_grad)

    layer_out[...] = (dec[...].astype(F32) + summed(ro)).astype(BF16)
    total = stat_sum[2]
    for step in range(1, NZ):
        arrived(None, stat_got.at[2 + step], stat_sems, 2 + step, peers["c"])
        total += stat_got[2 + step]
    mean = to_column(jnp.where(y == 0, total[0:1], total[4:5])) / features
    inv = inverse[y][:, 0:1]
    input_grad[...] = (
        masked_own[...].astype(F32)
        + inv * summed(rn)
        - dec[...].astype(F32) * (inv * inv * inv) * mean
    ).astype(BF16)
    enc_grad[...] = summed(re).astype(BF16)
    for copy in loads[4:]:
        copy.wait()
    sends.finish()


def write_kernel(*refs):
    n = (len(refs) - 1) // 2
    sems = refs[-1]
    copies = [pltpu.make_async_copy(refs[i], refs[n + i], sems.at[i]) for i in range(n)]
    for copy in copies:
        copy.start()
    for copy in copies:
        copy.wait()


def write_out(results):
    hbm = pl.BlockSpec(memory_space=pl.ANY)
    return pl.pallas_call(
        write_kernel,
        out_shape=tuple(jax.ShapeDtypeStruct(r.shape, r.dtype) for r in results),
        in_specs=[hbm] * len(results),
        out_specs=(hbm,) * len(results),
        scratch_shapes=[pltpu.SemaphoreType.DMA((len(results),))],
        compiler_params=pltpu.CompilerParams(vmem_limit_bytes=60 * 2**20),
        name="write_out",
    )(*results)


def fast(
    dec_input,
    enc_output,
    query_weight,
    key_weight,
    value_weight,
    output_weight,
    cotangent,
    enc_lengths,
    dec_lengths,
):
    vmem = pl.BlockSpec(memory_space=pltpu.VMEM)
    smem = pl.BlockSpec(memory_space=pltpu.SMEM)
    hbm = pl.BlockSpec(memory_space=pl.ANY)
    dma = lambda *shape: pltpu.SemaphoreType.DMA(shape)
    scratch = [
        pltpu.VMEM((2048, 256), BF16),
        pltpu.VMEM((2048, 256), BF16),
        pltpu.VMEM((2048, 256), BF16),
        pltpu.VMEM((256, 2048), BF16),
        pltpu.VMEM((256, 256), BF16),
        pltpu.VMEM((3, 256, 2048), BF16),
        pltpu.VMEM((3, 256, 2048), BF16),
        pltpu.VMEM((3, 256, 2048), BF16),
        pltpu.VMEM((2048, 256), BF16),
        pltpu.VMEM((2048, 256), BF16),
        pltpu.VMEM((2048, 256), BF16),
        pltpu.VMEM((256, 2048), BF16),
        pltpu.VMEM((2, 256, 2048), BF16),
        pltpu.VMEM((2, 256, 128), F32),
        pltpu.VMEM((2, 256, 128), F32),
        pltpu.VMEM((4, 2, 256, 256), F32),
        pltpu.VMEM((4, 256, 256), F32),
        pltpu.VMEM((4, 2, 256, 256), BF16),
        pltpu.VMEM((2, 256, 2048), BF16),
        pltpu.VMEM((2, 256, 2048), BF16),
        pltpu.VMEM((2, 256, 2048), BF16),
        pltpu.VMEM((8, 256), F32),
        pltpu.VMEM((8, 256), F32),
        pltpu.VMEM((8, 256), F32),
        pltpu.VMEM((6, 8, 256), F32),
        pltpu.VMEM((3, 8, 256), F32),
        dma(2, 6),
        dma(2, 9),
        dma(14),
    ]
    for n in (2, 1, 1):
        scratch += [dma(2, count * n) for count in (3, 3, 2, 4, 8)]
    for rows in (False, False, True):
        n = 4 if rows else 2
        r, w, wz = (16, 2048, 4096) if rows else (256, 256, 256)
        scratch += [
            pltpu.VMEM((4 * n, r, w), BF16),
            pltpu.VMEM((2 * n, r, w), BF16),
            pltpu.VMEM((2 * n, r, w), BF16),
            pltpu.VMEM((n, r, w), BF16),
            pltpu.VMEM((n, r, w), BF16),
            pltpu.VMEM((NZ, r, wz), F32),
        ]
        scratch += [pltpu.VMEM((NZ - 1, r, wz), BF16)] * 2
        scratch += [dma(2, k) for k in (4 * n, 2 * n, n, NZ - 1)]
    shapes = ((256, 256), (256, 256), (16, 4096)) + ((2048, 256),) * 3 + ((256, 2048),)
    results = pl.pallas_call(
        kernel,
        out_shape=tuple(jax.ShapeDtypeStruct(shape, BF16) for shape in shapes),
        in_specs=[smem, smem, vmem, vmem, vmem, hbm, hbm, hbm, hbm],
        out_specs=(vmem,) * 3 + (hbm,) * 4,
        scratch_shapes=scratch,
        compiler_params=pltpu.CompilerParams(
            collective_id=0, has_side_effects=True, vmem_limit_bytes=58 * 2**20
        ),
        name="cross_attention",
    )(
        enc_lengths, dec_lengths, dec_input[0], enc_output[0], cotangent[0],
        query_weight, key_weight, value_weight, output_weight,
    )
    results = write_out(results)
    return tuple(out[None] for out in results[:3]) + tuple(results[3:])


def solution(mesh):
    in_specs = (
        P("dp", None, "mp"),
        P("dp", "mp", None),
        P("dp", "mp"),
        P("dp", "mp"),
        P("dp", "mp"),
        P("mp", "dp"),
        P("dp", None, "mp"),
        P("dp"),
        P("dp"),
    )
    out_specs = (
        P("dp", None, "mp"),
        P("dp", None, "mp"),
        P("dp", "mp", None),
        P("dp", "mp"),
        P("dp", "mp"),
        P("dp", "mp"),
        P("mp", "dp"),
    )
    program = fast if dict(mesh.shape) == {"dp": 2, "mp": 16} else local
    return jax.shard_map(program, mesh=mesh, in_specs=in_specs, out_specs=out_specs, check_vma=False)
```

```python
import functools

import functools

import jax
import jax.numpy as jnp
from jax import lax
from jax.experimental import pallas as pl
from jax.experimental.pallas import tpu as pltpu
from jax.sharding import PartitionSpec as P

DH = 256
MESH = pl.DeviceIdType.MESH
F32 = jnp.float32
BF16 = jnp.bfloat16


def local(
    dec_input,
    enc_output,
    query_weight,
    key_weight,
    value_weight,
    output_weight,
    cotangent,
    enc_lengths,
    dec_lengths,
):
    scale = DH ** (-0.5)
    hidden = lax.all_gather(dec_input, "mp", axis=2, tiled=True)[0]
    query_full, key_full, value_full = (
        lax.all_gather(query_weight, "dp", axis=0, tiled=True),
        lax.all_gather(key_weight, "dp", axis=0, tiled=True),
        lax.all_gather(value_weight, "dp", axis=0, tiled=True),
    )
    output_full = lax.all_gather(output_weight, "dp", axis=1, tiled=True)
    encoded = lax.all_gather(enc_output, "mp", axis=1, tiled=True)[0]
    tokens = hidden.shape[0]
    keys_len = encoded.shape[0]
    width = query_weight.shape[1]
    heads_here = width // DH
    hidden32 = hidden.astype(jnp.float32)
    inv_rms = lax.rsqrt(jnp.mean(hidden32 * hidden32, axis=-1, keepdims=True) + 1e-06)
    normed = (hidden32 * inv_rms).astype(jnp.bfloat16)
    query = jnp.dot(normed, query_full, preferred_element_type=jnp.float32).astype(jnp.bfloat16)
    keyed = jnp.dot(encoded, key_full, preferred_element_type=jnp.float32).astype(jnp.bfloat16)
    valued = jnp.dot(encoded, value_full, preferred_element_type=jnp.float32).astype(jnp.bfloat16)
    query_heads = query.reshape(tokens, heads_here, DH)
    key_heads = keyed.reshape(keys_len, heads_here, DH)
    value_heads = valued.reshape(keys_len, heads_here, DH)
    scores = (
        jnp.einsum("thd,lhd->htl", query_heads, key_heads, preferred_element_type=jnp.float32)
        * scale
    )
    valid = jnp.arange(keys_len, dtype=jnp.int32) < enc_lengths[0]
    scores = jnp.where(valid[None, None, :], scores, -1e30)
    shifted = jnp.exp(scores - jnp.max(scores, axis=-1, keepdims=True))
    probs = shifted / jnp.sum(shifted, axis=-1, keepdims=True)
    probs_low = probs.astype(jnp.bfloat16)
    attended = (
        jnp.einsum("htl,lhd->thd", probs_low, value_heads, preferred_element_type=jnp.float32)
        .reshape(tokens, width)
        .astype(jnp.bfloat16)
    )
    partial_out = jnp.dot(attended, output_full, preferred_element_type=jnp.float32)
    out_share = lax.psum_scatter(
        partial_out.astype(jnp.bfloat16), "mp", scatter_dimension=1, tiled=True
    ).astype(jnp.float32)
    own_input = dec_input[0].astype(jnp.float32)
    layer_out = (own_input + out_share).astype(jnp.bfloat16)[None]
    upstream = lax.all_gather(cotangent, "mp", axis=2, tiled=True)[0]
    keep = (jnp.arange(tokens, dtype=jnp.int32) < dec_lengths[0])[:, None]
    masked = jnp.where(keep, upstream, jnp.zeros_like(upstream))
    own_masked = jnp.where(keep, cotangent[0], jnp.zeros_like(cotangent[0]))
    attended_grad = jnp.dot(masked, output_full.T, preferred_element_type=jnp.float32).astype(
        jnp.bfloat16
    )
    grad_heads = attended_grad.reshape(tokens, heads_here, DH)
    probs_grad = jnp.einsum(
        "thd,lhd->htl", grad_heads, value_heads, preferred_element_type=jnp.float32
    )
    scores_grad = (
        probs * (probs_grad - jnp.sum(probs * probs_grad, axis=-1, keepdims=True)) * scale
    ).astype(jnp.bfloat16)
    q_grad = (
        jnp.einsum("htl,lhd->thd", scores_grad, key_heads, preferred_element_type=jnp.float32)
        .reshape(tokens, width)
        .astype(jnp.bfloat16)
    )
    k_grad = (
        jnp.einsum("htl,thd->lhd", scores_grad, query_heads, preferred_element_type=jnp.float32)
        .reshape(keys_len, width)
        .astype(jnp.bfloat16)
    )
    v_grad = (
        jnp.einsum("htl,thd->lhd", probs_low, grad_heads, preferred_element_type=jnp.float32)
        .reshape(keys_len, width)
        .astype(jnp.bfloat16)
    )
    normed_part = jnp.dot(q_grad, query_full.T, preferred_element_type=jnp.float32)
    feature_width = dec_input.shape[2]
    normed_grad = lax.psum(normed_part.astype(jnp.bfloat16), "mp").astype(jnp.float32)
    stat = jnp.mean(normed_grad * hidden32, axis=-1, keepdims=True)
    full_grad = inv_rms * normed_grad - hidden32 * inv_rms**3 * stat
    start = lax.axis_index("mp") * feature_width
    input_share = lax.dynamic_slice_in_dim(full_grad, start, feature_width, 1)
    input_grad = (own_masked.astype(jnp.float32) + input_share).astype(jnp.bfloat16)[None]
    enc_share = lax.psum_scatter(
        (
            jnp.dot(k_grad, key_full.T, preferred_element_type=jnp.float32)
            + jnp.dot(v_grad, value_full.T, preferred_element_type=jnp.float32)
        ).astype(jnp.bfloat16),
        "mp",
        scatter_dimension=0,
        tiled=True,
    )
    enc_grad = enc_share[None]
    weight_share = lax.psum_scatter(
        jnp.concatenate(
            [
                jnp.dot(normed.T, q_grad, preferred_element_type=jnp.float32),
                jnp.dot(encoded.T, k_grad, preferred_element_type=jnp.float32),
                jnp.dot(encoded.T, v_grad, preferred_element_type=jnp.float32),
                jnp.dot(masked.T, attended, preferred_element_type=jnp.float32),
            ],
            axis=1,
        ).astype(jnp.bfloat16),
        "dp",
        scatter_dimension=0,
        tiled=True,
    ).astype(jnp.float32)
    query_grad = weight_share[:, :width].astype(jnp.bfloat16)
    key_grad = weight_share[:, width : 2 * width].astype(jnp.bfloat16)
    value_grad = weight_share[:, 2 * width : 3 * width].astype(jnp.bfloat16)
    output_grad = weight_share[:, 3 * width :].T.astype(jnp.bfloat16)
    return (layer_out, input_grad, enc_grad, query_grad, key_grad, value_grad, output_grad)


NZ = 4


def place():
    y, m = lax.axis_index("dp"), lax.axis_index("mp")
    z, x, c = m // 4, (m // 2) % 2, m % 2
    peers = {
        "up": (y, m + 4),
        "down": (y, m - 4),
        "y": (1 - y, m),
        "x": (y, m + 2 - 4 * x),
        "c": (y, m + 1 - 2 * c),
    }
    return y, z, x, c, peers


def when(pred, act):
    if pred is None:
        act()
    else:
        pl.when(pred)(act)


def both(a, b):
    return b if a is None else a if b is None else jnp.logical_and(a, b)


class Sends:
    def __init__(self):
        self.open = []

    def start(self, pred, src, dst, sems, at, peer):
        copy = pltpu.make_async_remote_copy(
            src_ref=src,
            dst_ref=dst,
            send_sem=sems.at[0, at],
            recv_sem=sems.at[1, at],
            device_id=peer,
            device_id_type=MESH,
        )
        when(pred, lambda: copy.start())
        self.open.append((pred, copy))

    def finish(self):
        for pred, copy in self.open:
            when(pred, lambda copy=copy: copy.wait_send())


def arrived(pred, dst, sems, at, peer):
    copy = pltpu.make_async_remote_copy(
        src_ref=dst,
        dst_ref=dst,
        send_sem=sems.at[0, at],
        recv_sem=sems.at[1, at],
        device_id=peer,
        device_id_type=MESH,
    )
    when(pred, lambda: copy.wait_recv())


def feature_block(ref, s, j, x, c):
    return ref.at[s, :, pl.ds(pl.multiple_of(j * 1024 + x * 512 + c * 256, 256), 256)]


def row_block(ref, s, j, x, c):
    return ref.at[s, pl.ds(pl.multiple_of(j * 64 + x * 32 + c * 16, 16), 16), :]


def line_peer(y, z, x, c, d):
    return (y, ((z + d) % NZ) * 4 + x * 2 + c)


def greet(here, peers):
    barrier = pltpu.get_barrier_semaphore()
    targets = [peers[way] for way in ("y", "x", "c")]
    targets += [line_peer(*here, d) for d in range(1, NZ)]
    for target in targets:
        pl.semaphore_signal(barrier, inc=1, device_id=target, device_id_type=MESH)
    pl.semaphore_wait(barrier, len(targets))


def matmul(a, b, dims=((1,), (0,))):
    return lax.dot_general(a, b, (dims, ((), ())), preferred_element_type=F32)


BY_ROWS = ((1,), (1,))
BY_TOKENS = ((0,), (0,))


def chunk(i, size):
    return pl.ds(pl.multiple_of(i * size, size), size)


def diagonal():
    return lax.broadcasted_iota(jnp.int32, (256, 256), 0) == lax.broadcasted_iota(
        jnp.int32, (256, 256), 1
    )


def to_row(column):
    return jnp.sum(jnp.where(diagonal(), column, 0.0), axis=0, keepdims=True)


def to_column(row):
    return jnp.sum(jnp.where(diagonal(), row, 0.0), axis=1, keepdims=True)


def two_rows(first, second):
    upper = lax.broadcasted_iota(jnp.int32, (8, 256), 0) < 4
    return jnp.where(upper, first, second)


GATHER_SEMS, REDUCE_REFS = 5, 12


def kernel(
    enc_len, dec_len, dec, enc, cot, wq_hbm, wk_hbm, wv_hbm, wo_hbm,
    layer_out, input_grad, enc_grad, query_out, key_out, value_out, output_out,
    query_grad, key_grad, value_grad, output_grad, masked_own, gd, ge, gc, wq, wk, wv, wo, normed, column, inverse,
    parts, parts_got, grads, po, ng, eg, squares, squares_got, stat,
    stat_got, stat_sum, stat_sems, swap_sems, local_sems, *scratch,
):
    y, z, x, c, peers = place()
    here = (y, z, x, c)
    sends = Sends()

    loads = []
    for i, (src, dst) in enumerate(((wk_hbm, wk), (wv_hbm, wv), (wq_hbm, wq), (wo_hbm, wo))):
        copy = pltpu.make_async_copy(src, dst, local_sems.at[i])
        copy.start()
        loads.append(copy)
    token = lax.broadcasted_iota(jnp.int32, (256, 256), 0)
    masked_own[...] = jnp.where(token < dec_len[0], cot[...].astype(F32), 0.0).astype(BF16)

    gathers = []
    for t, (own, out, rows) in enumerate(((enc, ge, True), (dec, gd, False), (masked_own, gc, False))):
        gathers.append((t, own, out, rows) + tuple(scratch[GATHER_SEMS * t : GATHER_SEMS * (t + 1)]))
    scratch = scratch[3 * GATHER_SEMS :]
    local = [[], [], []]

    def held(tensor, zz):
        _, own, out, rows = tensor[:4]
        if rows:
            return [row_block(out, y, zz, x, c), row_block(out, 2, zz, x, c)]
        slot = y + (2 - y) * ((zz // 2 + y) % 2)
        return [feature_block(out, slot, zz % 2, x, c)]

    def onward(tensor, zz, pred, own=None):
        t, _, out, rows, up, down, ys, xs, cs = tensor
        if rows:
            mine = row_block(out, y, zz, x, c)
            far = row_block(out, 2, zz, x, c)
            src, src_far = (mine, far) if own is None else own
            sends.start(pred, src_far, mine, ys, zz, peers["y"])
            sends.start(pred, src, mine, xs, y * 4 + zz, peers["x"])
            sends.start(pred, src, mine, cs, (y * 4 + zz) * 2 + x, peers["c"])
            return
        other = (zz // 2 + y) % 2
        j = zz % 2
        slot = y + (2 - y) * other
        src = feature_block(out, slot, j, x, c) if own is None else own[0]
        mine = feature_block(out, y, j, x, c)
        sends.start(both(pred, other == 1), src, mine, ys, j, peers["y"])
        near = both(pred, other == 0)
        sends.start(near, src, mine, xs, y * 2 + j, peers["x"])
        sends.start(near, src, mine, cs, (y * 2 + j) * 2 + x, peers["c"])

    def gather_start(tensor):
        t, own, out, rows, up, down = tensor[:6]
        views = held(tensor, z)
        srcs = [own]
        if rows:
            srcs = [own.at[:, chunk(y, 2048)], own.at[:, chunk(1 - y, 2048)]]
        for i, (src, view) in enumerate(zip(srcs, views)):
            sends.start(z < NZ - 1, src, view, up, i, peers["up"])
            sends.start(z > 0, src, view, down, i, peers["down"])
        onward(tensor, z, None, srcs)
        for i, (src, view) in enumerate(zip(srcs, views)):
            copy = pltpu.make_async_copy(src, view, local_sems.at[4 + 2 * t + i])
            copy.start()
            local[t].append(copy)

    def gather_z(tensor):
        t, own, out, rows, up, down = tensor[:6]
        for k in range(NZ - 1):
            below, above = z - 1 - k, z + 1 + k
            for zz, ok, sems_way, way, more in (
                (jnp.maximum(below, 0), below >= 0, up, "up", z < NZ - 1),
                (jnp.minimum(above, NZ - 1), above < NZ, down, "down", z > 0),
            ):
                views = held(tensor, zz)
                n = len(views)
                for i, view in enumerate(views):
                    arrived(ok, view, sems_way, k * n + i, peers["c"])
                    if k + 1 < NZ - 1:
                        sends.start(both(ok, more), view, view, sems_way, (k + 1) * n + i, peers[way])
                onward(tensor, zz, ok)

    def gather_y(tensor):
        t, own, out, rows, up, down, ys, xs, cs = tensor
        block, n = (row_block, 4) if rows else (feature_block, 2)
        for j in range(n):
            view = block(out, 1 - y, j, x, c)
            arrived(None, view, ys, j, peers["y"])
            sends.start(None, view, view, xs, (1 - y) * n + j, peers["x"])
            sends.start(None, view, view, cs, ((1 - y) * n + j) * 2 + x, peers["c"])

    def gather_x(tensor):
        t, own, out, rows, up, down, ys, xs, cs = tensor
        block, n = (row_block, 4) if rows else (feature_block, 2)
        for s in (y, 1 - y):
            for j in range(n):
                view = block(out, s, j, 1 - x, c)
                arrived(None, view, xs, s * n + j, peers["x"])
                sends.start(None, view, view, cs, (s * n + j) * 2 + 1 - x, peers["c"])

    def gather_c(tensor):
        t, own, out, rows, up, down, ys, xs, cs = tensor
        block, n = (row_block, 4) if rows else (feature_block, 2)
        for s in range(2):
            for j in range(n):
                for xx in range(2):
                    arrived(None, block(out, s, j, xx, 1 - c), cs, (s * n + j) * 2 + xx, peers["c"])
        for copy in local[t]:
            copy.wait()

    def project(i, left, weight, dims=((1,), (0,))):
        for s in (1 - y, y):
            parts[i, s] = matmul(left[s], weight[...], dims)
            if s is not y:
                sends.start(None, parts.at[i, s], parts_got.at[i], swap_sems, i, peers["y"])

    def projected(i):
        arrived(None, parts_got.at[i], swap_sems, i, peers["y"])
        return (parts[i, y] + parts_got[i]).astype(BF16)

    greet(here, peers)
    e, d, g = gathers
    gather_start(e)
    gather_start(d)
    gather_z(e)
    gather_start(g)
    gather_y(e)
    gather_z(d)
    gather_x(e)
    gather_y(d)
    gather_z(g)
    gather_c(e)
    loads[0].wait()
    project(0, ge, wk)
    gather_x(d)
    gather_y(g)
    gather_c(d)

    @pl.loop(0, 16)
    def _(i):
        s, rows = i // 8, chunk(i % 8, 32)
        value = gd[s, rows, :].astype(F32)
        total = jnp.sum(value * value, axis=-1, keepdims=True)
        column[s, rows, :] = jnp.broadcast_to(total, (32, 128))

    squares[...] = two_rows(to_row(column[0, :, 0:1]), to_row(column[1, :, 0:1]))
    sends.start(None, squares, squares_got, swap_sems, 8, peers["y"])
    loads[1].wait()
    project(1, ge, wv)
    arrived(None, squares_got, swap_sems, 8, peers["y"])
    features = 16 * dec.shape[1]
    inv_rows = lax.rsqrt((squares[...] + squares_got[...]) / features + 1e-06)
    for s in range(2):
        inverse[s] = jnp.broadcast_to(to_column(inv_rows[4 * s : 4 * s + 1]), (256, 128))

    @pl.loop(0, 16)
    def _(i):
        s, rows = i // 8, chunk(i % 8, 32)
        value = gd[s, rows, :].astype(F32) * inverse[s, rows, 0:1]
        normed[s, rows, :] = value.astype(BF16)

    loads[2].wait()
    project(2, normed, wq)
    gather_x(g)

    ATT, QG, KG, VG = range(4)

    def share(i, value):
        grads[i, y] = value.astype(BF16)
        sends.start(None, grads.at[i, y], grads.at[i, y], swap_sems, 4 + i, peers["y"])

    def shared(i):
        arrived(None, grads.at[i, 1 - y], swap_sems, 4 + i, peers["y"])

    scale = DH ** (-0.5)
    keyed = projected(0)
    query = projected(2)
    scores = matmul(query, keyed, BY_ROWS) * scale
    position = lax.broadcasted_iota(jnp.int32, (256, 256), 1)
    scores = jnp.where(position < enc_len[0], scores, -1e30)
    shifted = jnp.exp(scores - jnp.max(scores, axis=-1, keepdims=True))
    probs = shifted / jnp.sum(shifted, axis=-1, keepdims=True)
    probs_low = probs.astype(BF16)
    valued = projected(1)
    share(ATT, matmul(probs_low, valued))
    gather_c(g)
    loads[3].wait()
    project(3, gc, wo, BY_ROWS)

    reduces = []
    for t, (part, rows) in enumerate(((po, False), (ng, False), (eg, True))):
        reduces.append((part, rows) + tuple(scratch[REDUCE_REFS * t : REDUCE_REFS * (t + 1)]))

    def across_core(tensor, s):
        part, rows, rc, ax, rx, by, ry, v, sz, rz, cs, xs, ys, zs = tensor
        block, n = (row_block, 4) if rows else (feature_block, 2)
        for xx in (1 - x, x):
            for j in range(n):
                at = (s * n + j) * 2 + xx
                sends.start(None, block(part, s, j, xx, 1 - c), rc.at[at], cs, at, peers["c"])

    def across_x(tensor, s):
        part, rows, rc, ax, rx, by, ry, v, sz, rz, cs, xs, ys, zs = tensor
        block, n = (row_block, 4) if rows else (feature_block, 2)
        for j in range(n):
            at = (s * n + j) * 2 + 1 - x
            arrived(None, rc.at[at], cs, at, peers["c"])
            own = block(part, s, j, 1 - x, c)[...].astype(F32)
            ax[s * n + j] = (own + rc[at].astype(F32)).astype(BF16)
            sends.start(None, ax.at[s * n + j], rx.at[s * n + j], xs, s * n + j, peers["x"])

    def across_y(tensor, theirs):
        part, rows, rc, ax, rx, by, ry, v, sz, rz, cs, xs, ys, zs = tensor
        block, n = (row_block, 4) if rows else (feature_block, 2)
        s = 1 - y if theirs else y
        for j in range(n):
            at = (s * n + j) * 2 + x
            arrived(None, rc.at[at], cs, at, peers["c"])
            arrived(None, rx.at[s * n + j], xs, s * n + j, peers["x"])
            own = block(part, s, j, x, c)[...].astype(F32)
            total = own + rc[at].astype(F32) + rx[s * n + j].astype(F32)
            if theirs:
                by[j] = total.astype(BF16)
                sends.start(None, by.at[j], ry.at[j], ys, j, peers["y"])
            elif rows:
                v[j, :, chunk(y, 2048)] = total
            else:
                v[2 * y + j] = total

    def along_z(tensor):
        part, rows, rc, ax, rx, by, ry, v, sz, rz, cs, xs, ys, zs = tensor
        n = 4 if rows else 2
        for j in range(n):
            arrived(None, ry.at[j], ys, j, peers["y"])
            if rows:
                v[j, :, chunk(1 - y, 2048)] = ry[j].astype(F32)
            else:
                v[2 * (1 - y) + j] = ry[j].astype(F32)
        for step in (2, 1, 3):
            sz[step - 1] = v[(z + step) % NZ].astype(BF16)
            sends.start(
                None, sz.at[step - 1], rz.at[step - 1], zs, step - 1, line_peer(*here, step)
            )

    def summed(tensor):
        part, rows, rc, ax, rx, by, ry, v, sz, rz, cs, xs, ys, zs = tensor
        total = v[z]
        for step in range(1, NZ):
            arrived(None, rz.at[step - 1], zs, step - 1, peers["c"])
            total += rz[step - 1].astype(F32)
        return total

    def stat_step(k, way):
        arrived(None, stat_got.at[k], stat_sems, k, peers["c"])
        before = stat[...] if k == 0 else stat_sum[k - 1]
        stat_sum[k] = before + stat_got[k]
        if way:
            sends.start(None, stat_sum.at[k], stat_got.at[k + 1], stat_sems, k + 1, peers[way])

    def emit(i, value):
        out = (output_out, query_out, key_out, value_out)[i]
        copy = pltpu.make_async_copy(value, out, local_sems.at[10 + i])
        copy.start()
        loads.append(copy)

    def out_parts(s):
        @pl.loop(0, 4)
        def _(i):
            po[s, :, chunk(i, 512)] = matmul(grads[ATT, s], wo[:, chunk(i, 512)]).astype(BF16)

    def normed_parts(s):
        column[s] = jnp.zeros((256, 128), F32)

        @pl.loop(0, 8)
        def _(i):
            cols = chunk(i, 256)
            part = matmul(grads[QG, s], wq[cols, :], BY_ROWS).astype(BF16)
            ng[s, :, cols] = part
            dots = jnp.sum(part.astype(F32) * gd[s, :, cols].astype(F32), axis=-1, keepdims=True)
            column[s] += jnp.broadcast_to(dots, (256, 128))

    def enc_parts(s):
        @pl.loop(0, 4)
        def _(i):
            cols = chunk(i, 512)
            total = matmul(grads[KG, s], wk[cols, :], BY_ROWS)
            total += matmul(grads[VG, s], wv[cols, :], BY_ROWS)
            eg[s, :, cols] = total.astype(BF16)

    def weight_part(out, left, i):
        @pl.loop(0, 8)
        def _(step):
            rows = chunk(step, 256)
            total = matmul(left[0, :, rows], grads[i, 0], BY_TOKENS)
            total += matmul(left[1, :, rows], grads[i, 1], BY_TOKENS)
            out[rows, :] = total.astype(BF16)

        emit(i, out)

    ro, rn, re = reduces
    out_parts(y)
    across_core(ro, y)
    shared(ATT)
    out_parts(1 - y)
    across_core(ro, 1 - y)
    across_x(ro, y)
    across_x(ro, 1 - y)

    attended_grad = projected(3)
    probs_grad = matmul(attended_grad, valued, BY_ROWS)
    scores_grad = (
        probs * (probs_grad - jnp.sum(probs * probs_grad, axis=-1, keepdims=True)) * scale
    ).astype(BF16)
    share(QG, matmul(scores_grad, keyed))
    share(KG, matmul(scores_grad, query, BY_TOKENS))
    share(VG, matmul(probs_low, attended_grad, BY_TOKENS))
    normed_parts(y)
    across_core(rn, y)
    enc_parts(y)
    across_core(re, y)
    across_x(rn, y)
    shared(QG)
    normed_parts(1 - y)
    across_core(rn, 1 - y)
    stat[...] = two_rows(to_row(column[0, :, 0:1]), to_row(column[1, :, 0:1]))
    sends.start(None, stat, stat_got.at[0], stat_sems, 0, peers["c"])
    across_x(re, y)
    shared(KG)
    shared(VG)
    enc_parts(1 - y)
    across_core(re, 1 - y)
    across_x(rn, 1 - y)
    across_y(ro, True)
    across_y(ro, False)
    stat_step(0, "x")
    across_x(re, 1 - y)
    along_z(ro)
    weight_part(query_grad, normed, QG)
    stat_step(1, "y")
    weight_part(key_grad, ge, KG)
    across_y(rn, True)
    across_y(rn, False)
    stat_step(2, None)
    for step in range(1, NZ):
        sends.start(
            None, stat_sum.at[2], stat_got.at[2 + step], stat_sems, 2 + step, line_peer(*here, step)
        )
    along_z(rn)
    weight_part(value_grad, ge, VG)
    across_y(re, True)
    across_y(re, False)
    along_z(re)

    @pl.loop(0, 4)
    def _(i):
        cols = chunk(i, 512)
        total = matmul(grads[ATT, 0], gc[0, :, cols], BY_TOKENS)
        total += matmul(grads[ATT, 1], gc[1, :, cols], BY_TOKENS)
        output_grad[:, cols] = total.astype(BF16)

    emit(ATT, output_grad)

    layer_out[...] = (dec[...].astype(F32) + summed(ro)).astype(BF16)
    total = stat_sum[2]
    for step in range(1, NZ):
        arrived(None, stat_got.at[2 + step], stat_sems, 2 + step, peers["c"])
        total += stat_got[2 + step]
    mean = to_column(jnp.where(y == 0, total[0:1], total[4:5])) / features
    inv = inverse[y][:, 0:1]
    input_grad[...] = (
        masked_own[...].astype(F32)
        + inv * summed(rn)
        - dec[...].astype(F32) * (inv * inv * inv) * mean
    ).astype(BF16)
    enc_grad[...] = summed(re).astype(BF16)
    for copy in loads[4:]:
        copy.wait()
    sends.finish()


def write_kernel(n, *refs):
    sources, outs, held, sems = refs[:n], refs[n : 2 * n], refs[2 * n : 3 * n], refs[3 * n]
    reads = [pltpu.make_async_copy(sources[i], held[i], sems.at[i]) for i in range(n)]
    writes = [pltpu.make_async_copy(held[i], outs[i], sems.at[n + i]) for i in range(n)]
    for copy in reads:
        copy.start()
    for read, write in zip(reads, writes):
        read.wait()
        write.start()
    for copy in writes:
        copy.wait()


def write_out(results):
    hbm = pl.BlockSpec(memory_space=pl.ANY)
    return pl.pallas_call(
        functools.partial(write_kernel, len(results)),
        out_shape=tuple(jax.ShapeDtypeStruct(r.shape, r.dtype) for r in results),
        in_specs=[hbm] * len(results),
        out_specs=(hbm,) * len(results),
        scratch_shapes=[pltpu.VMEM(r.shape, r.dtype) for r in results]
        + [pltpu.SemaphoreType.DMA((2 * len(results),))],
        compiler_params=pltpu.CompilerParams(vmem_limit_bytes=60 * 2**20),
        name="write_out",
    )(*results)


def fast(
    dec_input,
    enc_output,
    query_weight,
    key_weight,
    value_weight,
    output_weight,
    cotangent,
    enc_lengths,
    dec_lengths,
):
    vmem = pl.BlockSpec(memory_space=pltpu.VMEM)
    smem = pl.BlockSpec(memory_space=pltpu.SMEM)
    hbm = pl.BlockSpec(memory_space=pl.ANY)
    dma = lambda *shape: pltpu.SemaphoreType.DMA(shape)
    scratch = [
        pltpu.VMEM((2048, 256), BF16),
        pltpu.VMEM((2048, 256), BF16),
        pltpu.VMEM((2048, 256), BF16),
        pltpu.VMEM((256, 2048), BF16),
        pltpu.VMEM((256, 256), BF16),
        pltpu.VMEM((3, 256, 2048), BF16),
        pltpu.VMEM((3, 256, 2048), BF16),
        pltpu.VMEM((3, 256, 2048), BF16),
        pltpu.VMEM((2048, 256), BF16),
        pltpu.VMEM((2048, 256), BF16),
        pltpu.VMEM((2048, 256), BF16),
        pltpu.VMEM((256, 2048), BF16),
        pltpu.VMEM((2, 256, 2048), BF16),
        pltpu.VMEM((2, 256, 128), F32),
        pltpu.VMEM((2, 256, 128), F32),
        pltpu.VMEM((4, 2, 256, 256), F32),
        pltpu.VMEM((4, 256, 256), F32),
        pltpu.VMEM((4, 2, 256, 256), BF16),
        pltpu.VMEM((2, 256, 2048), BF16),
        pltpu.VMEM((2, 256, 2048), BF16),
        pltpu.VMEM((2, 256, 2048), BF16),
        pltpu.VMEM((8, 256), F32),
        pltpu.VMEM((8, 256), F32),
        pltpu.VMEM((8, 256), F32),
        pltpu.VMEM((6, 8, 256), F32),
        pltpu.VMEM((3, 8, 256), F32),
        dma(2, 6),
        dma(2, 9),
        dma(14),
    ]
    for n in (2, 1, 1):
        scratch += [dma(2, count * n) for count in (3, 3, 2, 4, 8)]
    for rows in (False, False, True):
        n = 4 if rows else 2
        r, w, wz = (16, 2048, 4096) if rows else (256, 256, 256)
        scratch += [
            pltpu.VMEM((4 * n, r, w), BF16),
            pltpu.VMEM((2 * n, r, w), BF16),
            pltpu.VMEM((2 * n, r, w), BF16),
            pltpu.VMEM((n, r, w), BF16),
            pltpu.VMEM((n, r, w), BF16),
            pltpu.VMEM((NZ, r, wz), F32),
        ]
        scratch += [pltpu.VMEM((NZ - 1, r, wz), BF16)] * 2
        scratch += [dma(2, k) for k in (4 * n, 2 * n, n, NZ - 1)]
    shapes = ((256, 256), (256, 256), (16, 4096)) + ((2048, 256),) * 3 + ((256, 2048),)
    results = pl.pallas_call(
        kernel,
        out_shape=tuple(jax.ShapeDtypeStruct(shape, BF16) for shape in shapes),
        in_specs=[smem, smem, vmem, vmem, vmem, hbm, hbm, hbm, hbm],
        out_specs=(vmem,) * 3 + (hbm,) * 4,
        scratch_shapes=scratch,
        compiler_params=pltpu.CompilerParams(
            collective_id=0, has_side_effects=True, vmem_limit_bytes=58 * 2**20
        ),
        name="cross_attention",
    )(
        enc_lengths, dec_lengths, dec_input[0], enc_output[0], cotangent[0],
        query_weight, key_weight, value_weight, output_weight,
    )
    results = write_out(results)
    return tuple(out[None] for out in results[:3]) + tuple(results[3:])


def solution(mesh):
    in_specs = (
        P("dp", None, "mp"),
        P("dp", "mp", None),
        P("dp", "mp"),
        P("dp", "mp"),
        P("dp", "mp"),
        P("mp", "dp"),
        P("dp", None, "mp"),
        P("dp"),
        P("dp"),
    )
    out_specs = (
        P("dp", None, "mp"),
        P("dp", None, "mp"),
        P("dp", "mp", None),
        P("dp", "mp"),
        P("dp", "mp"),
        P("dp", "mp"),
        P("mp", "dp"),
    )
    program = fast if dict(mesh.shape) == {"dp": 2, "mp": 16} else local
    return jax.shard_map(program, mesh=mesh, in_specs=in_specs, out_specs=out_specs, check_vma=False)
```

```python
import functools

import functools

import jax
import jax.numpy as jnp
from jax import lax
from jax.experimental import pallas as pl
from jax.experimental.pallas import tpu as pltpu
from jax.sharding import PartitionSpec as P

DH = 256
MESH = pl.DeviceIdType.MESH
F32 = jnp.float32
BF16 = jnp.bfloat16


def local(
    dec_input,
    enc_output,
    query_weight,
    key_weight,
    value_weight,
    output_weight,
    cotangent,
    enc_lengths,
    dec_lengths,
):
    scale = DH ** (-0.5)
    hidden = lax.all_gather(dec_input, "mp", axis=2, tiled=True)[0]
    query_full, key_full, value_full = (
        lax.all_gather(query_weight, "dp", axis=0, tiled=True),
        lax.all_gather(key_weight, "dp", axis=0, tiled=True),
        lax.all_gather(value_weight, "dp", axis=0, tiled=True),
    )
    output_full = lax.all_gather(output_weight, "dp", axis=1, tiled=True)
    encoded = lax.all_gather(enc_output, "mp", axis=1, tiled=True)[0]
    tokens = hidden.shape[0]
    keys_len = encoded.shape[0]
    width = query_weight.shape[1]
    heads_here = width // DH
    hidden32 = hidden.astype(jnp.float32)
    inv_rms = lax.rsqrt(jnp.mean(hidden32 * hidden32, axis=-1, keepdims=True) + 1e-06)
    normed = (hidden32 * inv_rms).astype(jnp.bfloat16)
    query = jnp.dot(normed, query_full, preferred_element_type=jnp.float32).astype(jnp.bfloat16)
    keyed = jnp.dot(encoded, key_full, preferred_element_type=jnp.float32).astype(jnp.bfloat16)
    valued = jnp.dot(encoded, value_full, preferred_element_type=jnp.float32).astype(jnp.bfloat16)
    query_heads = query.reshape(tokens, heads_here, DH)
    key_heads = keyed.reshape(keys_len, heads_here, DH)
    value_heads = valued.reshape(keys_len, heads_here, DH)
    scores = (
        jnp.einsum("thd,lhd->htl", query_heads, key_heads, preferred_element_type=jnp.float32)
        * scale
    )
    valid = jnp.arange(keys_len, dtype=jnp.int32) < enc_lengths[0]
    scores = jnp.where(valid[None, None, :], scores, -1e30)
    shifted = jnp.exp(scores - jnp.max(scores, axis=-1, keepdims=True))
    probs = shifted / jnp.sum(shifted, axis=-1, keepdims=True)
    probs_low = probs.astype(jnp.bfloat16)
    attended = (
        jnp.einsum("htl,lhd->thd", probs_low, value_heads, preferred_element_type=jnp.float32)
        .reshape(tokens, width)
        .astype(jnp.bfloat16)
    )
    partial_out = jnp.dot(attended, output_full, preferred_element_type=jnp.float32)
    out_share = lax.psum_scatter(
        partial_out.astype(jnp.bfloat16), "mp", scatter_dimension=1, tiled=True
    ).astype(jnp.float32)
    own_input = dec_input[0].astype(jnp.float32)
    layer_out = (own_input + out_share).astype(jnp.bfloat16)[None]
    upstream = lax.all_gather(cotangent, "mp", axis=2, tiled=True)[0]
    keep = (jnp.arange(tokens, dtype=jnp.int32) < dec_lengths[0])[:, None]
    masked = jnp.where(keep, upstream, jnp.zeros_like(upstream))
    own_masked = jnp.where(keep, cotangent[0], jnp.zeros_like(cotangent[0]))
    attended_grad = jnp.dot(masked, output_full.T, preferred_element_type=jnp.float32).astype(
        jnp.bfloat16
    )
    grad_heads = attended_grad.reshape(tokens, heads_here, DH)
    probs_grad = jnp.einsum(
        "thd,lhd->htl", grad_heads, value_heads, preferred_element_type=jnp.float32
    )
    scores_grad = (
        probs * (probs_grad - jnp.sum(probs * probs_grad, axis=-1, keepdims=True)) * scale
    ).astype(jnp.bfloat16)
    q_grad = (
        jnp.einsum("htl,lhd->thd", scores_grad, key_heads, preferred_element_type=jnp.float32)
        .reshape(tokens, width)
        .astype(jnp.bfloat16)
    )
    k_grad = (
        jnp.einsum("htl,thd->lhd", scores_grad, query_heads, preferred_element_type=jnp.float32)
        .reshape(keys_len, width)
        .astype(jnp.bfloat16)
    )
    v_grad = (
        jnp.einsum("htl,thd->lhd", probs_low, grad_heads, preferred_element_type=jnp.float32)
        .reshape(keys_len, width)
        .astype(jnp.bfloat16)
    )
    normed_part = jnp.dot(q_grad, query_full.T, preferred_element_type=jnp.float32)
    feature_width = dec_input.shape[2]
    normed_grad = lax.psum(normed_part.astype(jnp.bfloat16), "mp").astype(jnp.float32)
    stat = jnp.mean(normed_grad * hidden32, axis=-1, keepdims=True)
    full_grad = inv_rms * normed_grad - hidden32 * inv_rms**3 * stat
    start = lax.axis_index("mp") * feature_width
    input_share = lax.dynamic_slice_in_dim(full_grad, start, feature_width, 1)
    input_grad = (own_masked.astype(jnp.float32) + input_share).astype(jnp.bfloat16)[None]
    enc_share = lax.psum_scatter(
        (
            jnp.dot(k_grad, key_full.T, preferred_element_type=jnp.float32)
            + jnp.dot(v_grad, value_full.T, preferred_element_type=jnp.float32)
        ).astype(jnp.bfloat16),
        "mp",
        scatter_dimension=0,
        tiled=True,
    )
    enc_grad = enc_share[None]
    weight_share = lax.psum_scatter(
        jnp.concatenate(
            [
                jnp.dot(normed.T, q_grad, preferred_element_type=jnp.float32),
                jnp.dot(encoded.T, k_grad, preferred_element_type=jnp.float32),
                jnp.dot(encoded.T, v_grad, preferred_element_type=jnp.float32),
                jnp.dot(masked.T, attended, preferred_element_type=jnp.float32),
            ],
            axis=1,
        ).astype(jnp.bfloat16),
        "dp",
        scatter_dimension=0,
        tiled=True,
    ).astype(jnp.float32)
    query_grad = weight_share[:, :width].astype(jnp.bfloat16)
    key_grad = weight_share[:, width : 2 * width].astype(jnp.bfloat16)
    value_grad = weight_share[:, 2 * width : 3 * width].astype(jnp.bfloat16)
    output_grad = weight_share[:, 3 * width :].T.astype(jnp.bfloat16)
    return (layer_out, input_grad, enc_grad, query_grad, key_grad, value_grad, output_grad)


NZ = 4


def place():
    y, m = lax.axis_index("dp"), lax.axis_index("mp")
    z, x, c = m // 4, (m // 2) % 2, m % 2
    peers = {
        "up": (y, m + 4),
        "down": (y, m - 4),
        "y": (1 - y, m),
        "x": (y, m + 2 - 4 * x),
        "c": (y, m + 1 - 2 * c),
    }
    return y, z, x, c, peers


def when(pred, act):
    if pred is None:
        act()
    else:
        pl.when(pred)(act)


def both(a, b):
    return b if a is None else a if b is None else jnp.logical_and(a, b)


class Sends:
    def __init__(self):
        self.open = []

    def start(self, pred, src, dst, sems, at, peer):
        copy = pltpu.make_async_remote_copy(
            src_ref=src,
            dst_ref=dst,
            send_sem=sems.at[0, at],
            recv_sem=sems.at[1, at],
            device_id=peer,
            device_id_type=MESH,
        )
        when(pred, lambda: copy.start())
        self.open.append((pred, copy))

    def finish(self):
        for pred, copy in self.open:
            when(pred, lambda copy=copy: copy.wait_send())


def arrived(pred, dst, sems, at, peer):
    copy = pltpu.make_async_remote_copy(
        src_ref=dst,
        dst_ref=dst,
        send_sem=sems.at[0, at],
        recv_sem=sems.at[1, at],
        device_id=peer,
        device_id_type=MESH,
    )
    when(pred, lambda: copy.wait_recv())


def feature_block(ref, s, j, x, c):
    return ref.at[s, :, pl.ds(pl.multiple_of(j * 1024 + x * 512 + c * 256, 256), 256)]


def row_block(ref, s, j, x, c):
    return ref.at[s, pl.ds(pl.multiple_of(j * 64 + x * 32 + c * 16, 16), 16), :]


def line_peer(y, z, x, c, d):
    return (y, ((z + d) % NZ) * 4 + x * 2 + c)


def greet(here, peers):
    barrier = pltpu.get_barrier_semaphore()
    targets = [peers[way] for way in ("y", "x", "c")]
    targets += [line_peer(*here, d) for d in range(1, NZ)]
    for target in targets:
        pl.semaphore_signal(barrier, inc=1, device_id=target, device_id_type=MESH)
    pl.semaphore_wait(barrier, len(targets))


def matmul(a, b, dims=((1,), (0,))):
    return lax.dot_general(a, b, (dims, ((), ())), preferred_element_type=F32)


BY_ROWS = ((1,), (1,))
BY_TOKENS = ((0,), (0,))


def chunk(i, size):
    return pl.ds(pl.multiple_of(i * size, size), size)


def diagonal():
    return lax.broadcasted_iota(jnp.int32, (256, 256), 0) == lax.broadcasted_iota(
        jnp.int32, (256, 256), 1
    )


def to_row(column):
    return jnp.sum(jnp.where(diagonal(), column, 0.0), axis=0, keepdims=True)


def to_column(row):
    return jnp.sum(jnp.where(diagonal(), row, 0.0), axis=1, keepdims=True)


def two_rows(first, second):
    upper = lax.broadcasted_iota(jnp.int32, (8, 256), 0) < 4
    return jnp.where(upper, first, second)


GATHER_SEMS, REDUCE_REFS = 5, 12


def kernel(
    enc_len, dec_len, dec, enc, cot, wq_hbm, wk_hbm, wv_hbm, wo_hbm,
    layer_out, input_grad, enc_grad, query_out, key_out, value_out, output_out,
    query_grad, key_grad, value_grad, output_grad, masked_own, gd, ge, gc, wq, wk, wv, wo, normed, column, inverse,
    parts, parts_got, grads, po, ng, eg, squares, squares_got, stat,
    stat_got, stat_sum, stat_sems, swap_sems, local_sems, *scratch,
):
    y, z, x, c, peers = place()
    here = (y, z, x, c)
    sends = Sends()

    loads = []
    for i, (src, dst) in enumerate(((wk_hbm, wk), (wv_hbm, wv), (wq_hbm, wq), (wo_hbm, wo))):
        copy = pltpu.make_async_copy(src, dst, local_sems.at[i])
        copy.start()
        loads.append(copy)
    token = lax.broadcasted_iota(jnp.int32, (256, 256), 0)
    masked_own[...] = jnp.where(token < dec_len[0], cot[...].astype(F32), 0.0).astype(BF16)

    gathers = []
    for t, (own, out, rows) in enumerate(((enc, ge, True), (dec, gd, False), (masked_own, gc, False))):
        gathers.append((t, own, out, rows) + tuple(scratch[GATHER_SEMS * t : GATHER_SEMS * (t + 1)]))
    scratch = scratch[3 * GATHER_SEMS :]
    local = [[], [], []]

    def held(tensor, zz):
        _, own, out, rows = tensor[:4]
        if rows:
            return [row_block(out, y, zz, x, c), row_block(out, 2, zz, x, c)]
        slot = y + (2 - y) * ((zz // 2 + y) % 2)
        return [feature_block(out, slot, zz % 2, x, c)]

    def onward(tensor, zz, pred, own=None):
        t, _, out, rows, up, down, ys, xs, cs = tensor
        if rows:
            mine = row_block(out, y, zz, x, c)
            far = row_block(out, 2, zz, x, c)
            src, src_far = (mine, far) if own is None else own
            sends.start(pred, src_far, mine, ys, zz, peers["y"])
            sends.start(pred, src, mine, xs, y * 4 + zz, peers["x"])
            sends.start(pred, src, mine, cs, (y * 4 + zz) * 2 + x, peers["c"])
            return
        other = (zz // 2 + y) % 2
        j = zz % 2
        slot = y + (2 - y) * other
        src = feature_block(out, slot, j, x, c) if own is None else own[0]
        mine = feature_block(out, y, j, x, c)
        sends.start(both(pred, other == 1), src, mine, ys, j, peers["y"])
        near = both(pred, other == 0)
        sends.start(near, src, mine, xs, y * 2 + j, peers["x"])
        sends.start(near, src, mine, cs, (y * 2 + j) * 2 + x, peers["c"])

    def gather_start(tensor):
        t, own, out, rows, up, down = tensor[:6]
        views = held(tensor, z)
        srcs = [own]
        if rows:
            srcs = [own.at[:, chunk(y, 2048)], own.at[:, chunk(1 - y, 2048)]]
        for i, (src, view) in enumerate(zip(srcs, views)):
            sends.start(z < NZ - 1, src, view, up, i, peers["up"])
            sends.start(z > 0, src, view, down, i, peers["down"])
        onward(tensor, z, None, srcs)
        for i, (src, view) in enumerate(zip(srcs, views)):
            copy = pltpu.make_async_copy(src, view, local_sems.at[4 + 2 * t + i])
            copy.start()
            local[t].append(copy)

    def gather_z(tensor):
        t, own, out, rows, up, down = tensor[:6]
        for k in range(NZ - 1):
            below, above = z - 1 - k, z + 1 + k
            for zz, ok, sems_way, way, more in (
                (jnp.maximum(below, 0), below >= 0, up, "up", z < NZ - 1),
                (jnp.minimum(above, NZ - 1), above < NZ, down, "down", z > 0),
            ):
                views = held(tensor, zz)
                n = len(views)
                for i, view in enumerate(views):
                    arrived(ok, view, sems_way, k * n + i, peers["c"])
                    if k + 1 < NZ - 1:
                        sends.start(both(ok, more), view, view, sems_way, (k + 1) * n + i, peers[way])
                onward(tensor, zz, ok)

    def gather_y(tensor):
        t, own, out, rows, up, down, ys, xs, cs = tensor
        block, n = (row_block, 4) if rows else (feature_block, 2)
        for j in range(n):
            view = block(out, 1 - y, j, x, c)
            arrived(None, view, ys, j, peers["y"])
            sends.start(None, view, view, xs, (1 - y) * n + j, peers["x"])
            sends.start(None, view, view, cs, ((1 - y) * n + j) * 2 + x, peers["c"])

    def gather_x(tensor):
        t, own, out, rows, up, down, ys, xs, cs = tensor
        block, n = (row_block, 4) if rows else (feature_block, 2)
        for s in (y, 1 - y):
            for j in range(n):
                view = block(out, s, j, 1 - x, c)
                arrived(None, view, xs, s * n + j, peers["x"])
                sends.start(None, view, view, cs, (s * n + j) * 2 + 1 - x, peers["c"])

    def gather_c(tensor):
        t, own, out, rows, up, down, ys, xs, cs = tensor
        block, n = (row_block, 4) if rows else (feature_block, 2)
        for s in range(2):
            for j in range(n):
                for xx in range(2):
                    arrived(None, block(out, s, j, xx, 1 - c), cs, (s * n + j) * 2 + xx, peers["c"])
        for copy in local[t]:
            copy.wait()

    def project(i, left, weight, dims=((1,), (0,))):
        for s in (1 - y, y):
            parts[i, s] = matmul(left[s], weight[...], dims)
            if s is not y:
                sends.start(None, parts.at[i, s], parts_got.at[i], swap_sems, i, peers["y"])

    def projected(i):
        arrived(None, parts_got.at[i], swap_sems, i, peers["y"])
        return (parts[i, y] + parts_got[i]).astype(BF16)

    greet(here, peers)
    e, d, g = gathers
    gather_start(e)
    gather_start(d)
    gather_z(e)
    gather_start(g)
    gather_y(e)
    gather_z(d)
    gather_x(e)
    gather_y(d)
    gather_z(g)
    gather_c(e)
    loads[0].wait()
    project(0, ge, wk)
    gather_x(d)
    gather_y(g)
    gather_c(d)

    @pl.loop(0, 16)
    def _(i):
        s, rows = i // 8, chunk(i % 8, 32)
        value = gd[s, rows, :].astype(F32)
        total = jnp.sum(value * value, axis=-1, keepdims=True)
        column[s, rows, :] = jnp.broadcast_to(total, (32, 128))

    squares[...] = two_rows(to_row(column[0, :, 0:1]), to_row(column[1, :, 0:1]))
    sends.start(None, squares, squares_got, swap_sems, 8, peers["y"])
    loads[1].wait()
    project(1, ge, wv)
    arrived(None, squares_got, swap_sems, 8, peers["y"])
    features = 16 * dec.shape[1]
    inv_rows = lax.rsqrt((squares[...] + squares_got[...]) / features + 1e-06)
    for s in range(2):
        inverse[s] = jnp.broadcast_to(to_column(inv_rows[4 * s : 4 * s + 1]), (256, 128))

    @pl.loop(0, 16)
    def _(i):
        s, rows = i // 8, chunk(i % 8, 32)
        value = gd[s, rows, :].astype(F32) * inverse[s, rows, 0:1]
        normed[s, rows, :] = value.astype(BF16)

    loads[2].wait()
    project(2, normed, wq)
    gather_x(g)

    ATT, QG, KG, VG = range(4)

    def share(i, value):
        grads[i, y] = value.astype(BF16)
        sends.start(None, grads.at[i, y], grads.at[i, y], swap_sems, 4 + i, peers["y"])

    def shared(i):
        arrived(None, grads.at[i, 1 - y], swap_sems, 4 + i, peers["y"])

    scale = DH ** (-0.5)
    keyed = projected(0)
    query = projected(2)
    scores = matmul(query, keyed, BY_ROWS) * scale
    position = lax.broadcasted_iota(jnp.int32, (256, 256), 1)
    scores = jnp.where(position < enc_len[0], scores, -1e30)
    shifted = jnp.exp(scores - jnp.max(scores, axis=-1, keepdims=True))
    probs = shifted / jnp.sum(shifted, axis=-1, keepdims=True)
    probs_low = probs.astype(BF16)
    valued = projected(1)
    share(ATT, matmul(probs_low, valued))
    gather_c(g)
    loads[3].wait()
    project(3, gc, wo, BY_ROWS)

    reduces = []
    for t, (part, rows) in enumerate(((po, False), (ng, False), (eg, True))):
        reduces.append((part, rows) + tuple(scratch[REDUCE_REFS * t : REDUCE_REFS * (t + 1)]))

    def across_core(tensor, s):
        part, rows, rc, ax, rx, by, ry, v, sz, rz, cs, xs, ys, zs = tensor
        block, n = (row_block, 4) if rows else (feature_block, 2)
        for xx in (1 - x, x):
            for j in range(n):
                at = (s * n + j) * 2 + xx
                sends.start(None, block(part, s, j, xx, 1 - c), rc.at[at], cs, at, peers["c"])

    def across_x(tensor, s):
        part, rows, rc, ax, rx, by, ry, v, sz, rz, cs, xs, ys, zs = tensor
        block, n = (row_block, 4) if rows else (feature_block, 2)
        for j in range(n):
            at = (s * n + j) * 2 + 1 - x
            arrived(None, rc.at[at], cs, at, peers["c"])
            own = block(part, s, j, 1 - x, c)[...].astype(F32)
            ax[s * n + j] = (own + rc[at].astype(F32)).astype(BF16)
            sends.start(None, ax.at[s * n + j], rx.at[s * n + j], xs, s * n + j, peers["x"])

    def across_y(tensor, theirs):
        part, rows, rc, ax, rx, by, ry, v, sz, rz, cs, xs, ys, zs = tensor
        block, n = (row_block, 4) if rows else (feature_block, 2)
        s = 1 - y if theirs else y
        for j in range(n):
            at = (s * n + j) * 2 + x
            arrived(None, rc.at[at], cs, at, peers["c"])
            arrived(None, rx.at[s * n + j], xs, s * n + j, peers["x"])
            own = block(part, s, j, x, c)[...].astype(F32)
            total = own + rc[at].astype(F32) + rx[s * n + j].astype(F32)
            if theirs:
                by[j] = total.astype(BF16)
                sends.start(None, by.at[j], ry.at[j], ys, j, peers["y"])
            elif rows:
                v[j, :, chunk(y, 2048)] = total
            else:
                v[2 * y + j] = total

    def along_z(tensor):
        part, rows, rc, ax, rx, by, ry, v, sz, rz, cs, xs, ys, zs = tensor
        n = 4 if rows else 2
        for j in range(n):
            arrived(None, ry.at[j], ys, j, peers["y"])
            if rows:
                v[j, :, chunk(1 - y, 2048)] = ry[j].astype(F32)
            else:
                v[2 * (1 - y) + j] = ry[j].astype(F32)
        for step in (2, 1, 3):
            sz[step - 1] = v[(z + step) % NZ].astype(BF16)
            sends.start(
                None, sz.at[step - 1], rz.at[step - 1], zs, step - 1, line_peer(*here, step)
            )

    def summed(tensor):
        part, rows, rc, ax, rx, by, ry, v, sz, rz, cs, xs, ys, zs = tensor
        total = v[z]
        for step in range(1, NZ):
            arrived(None, rz.at[step - 1], zs, step - 1, peers["c"])
            total += rz[step - 1].astype(F32)
        return total

    def stat_step(k, way):
        arrived(None, stat_got.at[k], stat_sems, k, peers["c"])
        before = stat[...] if k == 0 else stat_sum[k - 1]
        stat_sum[k] = before + stat_got[k]
        if way:
            sends.start(None, stat_sum.at[k], stat_got.at[k + 1], stat_sems, k + 1, peers[way])

    def emit(i, value):
        out = (output_out, query_out, key_out, value_out)[i]
        copy = pltpu.make_async_copy(value, out, local_sems.at[10 + i])
        copy.start()
        loads.append(copy)

    def out_parts(s):
        @pl.loop(0, 4)
        def _(i):
            po[s, :, chunk(i, 512)] = matmul(grads[ATT, s], wo[:, chunk(i, 512)]).astype(BF16)

    def normed_parts(s):
        column[s] = jnp.zeros((256, 128), F32)

        @pl.loop(0, 8)
        def _(i):
            cols = chunk(i, 256)
            part = matmul(grads[QG, s], wq[cols, :], BY_ROWS).astype(BF16)
            ng[s, :, cols] = part
            dots = jnp.sum(part.astype(F32) * gd[s, :, cols].astype(F32), axis=-1, keepdims=True)
            column[s] += jnp.broadcast_to(dots, (256, 128))

    def enc_parts(s):
        @pl.loop(0, 4)
        def _(i):
            cols = chunk(i, 512)
            total = matmul(grads[KG, s], wk[cols, :], BY_ROWS)
            total += matmul(grads[VG, s], wv[cols, :], BY_ROWS)
            eg[s, :, cols] = total.astype(BF16)

    def weight_part(out, left, i):
        @pl.loop(0, 8)
        def _(step):
            rows = chunk(step, 256)
            total = matmul(left[0, :, rows], grads[i, 0], BY_TOKENS)
            total += matmul(left[1, :, rows], grads[i, 1], BY_TOKENS)
            out[rows, :] = total.astype(BF16)

        emit(i, out)

    ro, rn, re = reduces
    out_parts(y)
    across_core(ro, y)
    shared(ATT)
    out_parts(1 - y)
    across_core(ro, 1 - y)
    across_x(ro, y)
    across_x(ro, 1 - y)

    @pl.loop(0, 4)
    def _(i):
        cols = chunk(i, 512)
        total = matmul(grads[ATT, 0], gc[0, :, cols], BY_TOKENS)
        total += matmul(grads[ATT, 1], gc[1, :, cols], BY_TOKENS)
        output_grad[:, cols] = total.astype(BF16)

    emit(ATT, output_grad)

    attended_grad = projected(3)
    probs_grad = matmul(attended_grad, valued, BY_ROWS)
    scores_grad = (
        probs * (probs_grad - jnp.sum(probs * probs_grad, axis=-1, keepdims=True)) * scale
    ).astype(BF16)
    share(QG, matmul(scores_grad, keyed))
    share(KG, matmul(scores_grad, query, BY_TOKENS))
    share(VG, matmul(probs_low, attended_grad, BY_TOKENS))
    normed_parts(y)
    across_core(rn, y)
    enc_parts(y)
    across_core(re, y)
    across_x(rn, y)
    shared(QG)
    normed_parts(1 - y)
    across_core(rn, 1 - y)
    stat[...] = two_rows(to_row(column[0, :, 0:1]), to_row(column[1, :, 0:1]))
    sends.start(None, stat, stat_got.at[0], stat_sems, 0, peers["c"])
    across_x(re, y)
    shared(KG)
    shared(VG)
    enc_parts(1 - y)
    across_core(re, 1 - y)
    across_x(rn, 1 - y)
    across_y(ro, True)
    across_y(ro, False)
    stat_step(0, "x")
    across_x(re, 1 - y)
    along_z(ro)
    weight_part(query_grad, normed, QG)
    stat_step(1, "y")
    weight_part(key_grad, ge, KG)
    across_y(rn, True)
    across_y(rn, False)
    stat_step(2, None)
    for step in range(1, NZ):
        sends.start(
            None, stat_sum.at[2], stat_got.at[2 + step], stat_sems, 2 + step, line_peer(*here, step)
        )
    along_z(rn)
    across_y(re, True)
    across_y(re, False)
    along_z(re)
    weight_part(value_grad, ge, VG)

    layer_out[...] = (dec[...].astype(F32) + summed(ro)).astype(BF16)
    total = stat_sum[2]
    for step in range(1, NZ):
        arrived(None, stat_got.at[2 + step], stat_sems, 2 + step, peers["c"])
        total += stat_got[2 + step]
    mean = to_column(jnp.where(y == 0, total[0:1], total[4:5])) / features
    inv = inverse[y][:, 0:1]
    input_grad[...] = (
        masked_own[...].astype(F32)
        + inv * summed(rn)
        - dec[...].astype(F32) * (inv * inv * inv) * mean
    ).astype(BF16)
    enc_grad[...] = summed(re).astype(BF16)
    for copy in loads[4:]:
        copy.wait()
    sends.finish()


def write_kernel(n, *refs):
    sources, outs, held, sems = refs[:n], refs[n : 2 * n], refs[2 * n : 3 * n], refs[3 * n]
    reads = [pltpu.make_async_copy(sources[i], held[i], sems.at[i]) for i in range(n)]
    writes = [pltpu.make_async_copy(held[i], outs[i], sems.at[n + i]) for i in range(n)]
    for copy in reads:
        copy.start()
    for read, write in zip(reads, writes):
        read.wait()
        write.start()
    for copy in writes:
        copy.wait()


def write_out(results):
    hbm = pl.BlockSpec(memory_space=pl.ANY)
    return pl.pallas_call(
        functools.partial(write_kernel, len(results)),
        out_shape=tuple(jax.ShapeDtypeStruct(r.shape, r.dtype) for r in results),
        in_specs=[hbm] * len(results),
        out_specs=(hbm,) * len(results),
        scratch_shapes=[pltpu.VMEM(r.shape, r.dtype) for r in results]
        + [pltpu.SemaphoreType.DMA((2 * len(results),))],
        compiler_params=pltpu.CompilerParams(vmem_limit_bytes=60 * 2**20),
        name="write_out",
    )(*results)


def fast(
    dec_input,
    enc_output,
    query_weight,
    key_weight,
    value_weight,
    output_weight,
    cotangent,
    enc_lengths,
    dec_lengths,
):
    vmem = pl.BlockSpec(memory_space=pltpu.VMEM)
    smem = pl.BlockSpec(memory_space=pltpu.SMEM)
    hbm = pl.BlockSpec(memory_space=pl.ANY)
    dma = lambda *shape: pltpu.SemaphoreType.DMA(shape)
    scratch = [
        pltpu.VMEM((2048, 256), BF16),
        pltpu.VMEM((2048, 256), BF16),
        pltpu.VMEM((2048, 256), BF16),
        pltpu.VMEM((256, 2048), BF16),
        pltpu.VMEM((256, 256), BF16),
        pltpu.VMEM((3, 256, 2048), BF16),
        pltpu.VMEM((3, 256, 2048), BF16),
        pltpu.VMEM((3, 256, 2048), BF16),
        pltpu.VMEM((2048, 256), BF16),
        pltpu.VMEM((2048, 256), BF16),
        pltpu.VMEM((2048, 256), BF16),
        pltpu.VMEM((256, 2048), BF16),
        pltpu.VMEM((2, 256, 2048), BF16),
        pltpu.VMEM((2, 256, 128), F32),
        pltpu.VMEM((2, 256, 128), F32),
        pltpu.VMEM((4, 2, 256, 256), F32),
        pltpu.VMEM((4, 256, 256), F32),
        pltpu.VMEM((4, 2, 256, 256), BF16),
        pltpu.VMEM((2, 256, 2048), BF16),
        pltpu.VMEM((2, 256, 2048), BF16),
        pltpu.VMEM((2, 256, 2048), BF16),
        pltpu.VMEM((8, 256), F32),
        pltpu.VMEM((8, 256), F32),
        pltpu.VMEM((8, 256), F32),
        pltpu.VMEM((6, 8, 256), F32),
        pltpu.VMEM((3, 8, 256), F32),
        dma(2, 6),
        dma(2, 9),
        dma(14),
    ]
    for n in (2, 1, 1):
        scratch += [dma(2, count * n) for count in (3, 3, 2, 4, 8)]
    for rows in (False, False, True):
        n = 4 if rows else 2
        r, w, wz = (16, 2048, 4096) if rows else (256, 256, 256)
        scratch += [
            pltpu.VMEM((4 * n, r, w), BF16),
            pltpu.VMEM((2 * n, r, w), BF16),
            pltpu.VMEM((2 * n, r, w), BF16),
            pltpu.VMEM((n, r, w), BF16),
            pltpu.VMEM((n, r, w), BF16),
            pltpu.VMEM((NZ, r, wz), F32),
        ]
        scratch += [pltpu.VMEM((NZ - 1, r, wz), BF16)] * 2
        scratch += [dma(2, k) for k in (4 * n, 2 * n, n, NZ - 1)]
    shapes = ((256, 256), (256, 256), (16, 4096)) + ((2048, 256),) * 3 + ((256, 2048),)
    results = pl.pallas_call(
        kernel,
        out_shape=tuple(jax.ShapeDtypeStruct(shape, BF16) for shape in shapes),
        in_specs=[smem, smem, vmem, vmem, vmem, hbm, hbm, hbm, hbm],
        out_specs=(vmem,) * 3 + (hbm,) * 4,
        scratch_shapes=scratch,
        compiler_params=pltpu.CompilerParams(
            collective_id=0, has_side_effects=True, vmem_limit_bytes=58 * 2**20
        ),
        name="cross_attention",
    )(
        enc_lengths, dec_lengths, dec_input[0], enc_output[0], cotangent[0],
        query_weight, key_weight, value_weight, output_weight,
    )
    results = write_out(results)
    return tuple(out[None] for out in results[:3]) + tuple(results[3:])


def solution(mesh):
    in_specs = (
        P("dp", None, "mp"),
        P("dp", "mp", None),
        P("dp", "mp"),
        P("dp", "mp"),
        P("dp", "mp"),
        P("mp", "dp"),
        P("dp", None, "mp"),
        P("dp"),
        P("dp"),
    )
    out_specs = (
        P("dp", None, "mp"),
        P("dp", None, "mp"),
        P("dp", "mp", None),
        P("dp", "mp"),
        P("dp", "mp"),
        P("dp", "mp"),
        P("mp", "dp"),
    )
    program = fast if dict(mesh.shape) == {"dp": 2, "mp": 16} else local
    return jax.shard_map(program, mesh=mesh, in_specs=in_specs, out_specs=out_specs, check_vma=False)
```
